32 devices in a mesh: groups: 2 (over y), gx: 4 (over z), gy: 4 (over x, core).
Axes of the slice: x: 2, y: 2, z: 4, core: 2. Of those that a mesh axis runs over, the one named last changes fastest.
Arguments:
- activations: bfloat16 [128, 18432], P(('groups', 'gy'), 'gx'), parts along dimension 0, may hold values from -6 to 6
- ln_gain: bfloat16 [18432], P('gx'), may hold values from 0.099609375 to 1.8984375
- w_query: bfloat16 [18432, 12288], P('gx', 'gy'), may hold values from -0.046875 to 0.046875
- w_keyval: bfloat16 [18432, 512], P('gx'), may hold values from -0.046875 to 0.046875
- w_out: bfloat16 [12288, 18432], P('gy', 'gx'), may hold values from -0.0546875 to 0.0546875
- k_cache: bfloat16 [128, 1024, 256], P(('groups', 'gx', 'gy')), parts along dimension 0, may hold values from -4000 to 4000
- v_cache: bfloat16 [128, 1024, 256], P(('groups', 'gx', 'gy')), parts along dimension 0, may hold values from -24 to 24
- cache_lengths: int32 [128], P(('groups', 'gx', 'gy')), parts along dimension 0, may hold values from 1 to 1024, as said below
Outputs:
- attn_out: bfloat16 [128, 18432], P(('groups', 'gy'), 'gx'), parts along dimension 0
The draws below stay inside these ranges and needn't reach their ends.
There are 2 independent parts, one for each index of `groups`. The reference program is written for one: setup_inputs(seed, part) draws one part's arguments, and reference() takes and returns one part's arrays. A program takes and returns all parts, laid end to end along the dimension named above; an argument that names none is the same for every part. Nothing has to cross between parts.
Inputs may be any that keep to these rules, and one draw needn't show every extreme that they name: `cache_lengths`: some sequence uses all 1024 positions.
All inputs are finite; a program needn't handle non-finite values.
Results may differ from the reference program's by a relative error of at most 0.012.
The reference program's roundings to bfloat16 on the way (of `normed`, `queries`, `keyval`, `weights` and `attended`) count: a program that leaves them out, or rounds other values in their place, can miss the bound.
Values may be sent and summed in bfloat16 or wider, within the bound.
No kernel may reach another device: no remote copies, remote signals or barrier semaphores. Data moves between devices by JAX's collectives and lax.ppermute only.
A program may use at most 192 MiB of HBM per device.

```python
import jax
import jax.numpy as jnp
from jax import lax

D = 18432
HEADS = 48
HEAD_DIM = 256
CACHE = 1024
BATCH = 64
QWIDTH = 12288


def draw_k_cache(key, part):
    key = jax.random.fold_in(key, 11)
    first = jax.random.fold_in(key, 0)
    keys = jax.random.normal(first, (BATCH, CACHE, HEAD_DIM), jnp.float32)
    return keys.astype(jnp.bfloat16)


def draw_cache_lengths(key, part):
    key = jax.random.fold_in(key, 23)
    first, second = jax.random.split(key)
    raw = jax.random.randint(first, (BATCH,), 0, CACHE, jnp.int32)
    lengths = 1 + raw * raw // CACHE
    longest = jax.random.randint(second, (), 0, BATCH, jnp.int32)
    return lengths.at[longest].set(CACHE).astype(jnp.int32)


def block_scale(rng, extent, shards, smallest, top_value):
    level = 1.0
    for dim, parts in shards:
        draws = jax.random.uniform(jax.random.fold_in(jax.random.fold_in(rng, 6), dim), (parts,), jnp.float32, smallest / len(shards), top_value / len(shards))
        level = level * jnp.repeat(jnp.exp(draws), extent[dim] // parts).reshape((-1,) + (1,) * (len(extent) - 1 - dim))
    return level


def bell_draw(stream_key, shape, deviation, bound, pieces=(), dtype=jnp.bfloat16):
    loudness = block_scale(stream_key, shape, pieces, -0.22, 0.18) if pieces else 1.0
    entries = jax.random.normal(stream_key, shape, jnp.float32) * deviation * loudness
    return jnp.minimum(jnp.maximum(entries, -bound), bound).astype(dtype)


def setup_inputs(seed: int = 0, part: int = 0) -> dict:
    splits = jax.random.split(jax.random.key(seed), 9)
    own_keys = jax.random.split(jax.random.fold_in(splits[8], part), 9)
    activations = bell_draw(own_keys[0], (BATCH, D), 1.0, 6.0, ((0, 4), (1, 4)))
    ln_gain = jnp.clip(1.0 + 0.18 * jax.random.normal(splits[1], (D,), jnp.float32), 0.099609375, 1.8984375).astype(jnp.bfloat16)
    w_query = bell_draw(splits[2], (D, QWIDTH), D ** -0.5, 0.046875, ((0, 4), (1, 4)))
    w_keyval = bell_draw(splits[3], (D, 2 * HEAD_DIM), D ** -0.5, 0.046875, ((0, 4),))
    w_out = bell_draw(splits[4], (QWIDTH, D), QWIDTH ** -0.5, 0.0546875, ((0, 4), (1, 4)))
    k_cache = draw_k_cache(jax.random.fold_in(jax.random.fold_in(splits[8], part), 71), part)
    v_cache = bell_draw(own_keys[6], (BATCH, CACHE, HEAD_DIM), 4.0, 24.0, ((0, 16),))
    cache_lengths = draw_cache_lengths(jax.random.fold_in(jax.random.fold_in(splits[8], part), 71), part)
    return dict(activations=activations, ln_gain=ln_gain, w_query=w_query, w_keyval=w_keyval, w_out=w_out, k_cache=k_cache, v_cache=v_cache, cache_lengths=cache_lengths)


def attend_one(packed):
    query_rows, keys, values, length, new_key, new_value = packed
    query_f = query_rows.astype(jnp.float32)
    scores = jnp.einsum('hd,td->ht', query_f, keys.astype(jnp.float32)) * 0.0625
    new_score = jnp.einsum('hd,d->h', query_f, new_key.astype(jnp.float32)) * 0.0625
    positions = lax.broadcasted_iota(jnp.int32, (1, CACHE), 1)
    live = positions < length
    masked = jnp.where(live, scores, jnp.float32(-1e+30))
    top = jnp.maximum(lax.optimization_barrier(jnp.max(masked, axis=1)), new_score)
    expo = jnp.where(live, jnp.exp(masked - top[:, None]), jnp.float32(0.0))
    new_expo = jnp.exp(new_score - top)
    denom = lax.optimization_barrier(jnp.sum(expo, axis=1)) + new_expo
    weights = (expo / denom[:, None]).astype(jnp.bfloat16)
    new_weight = (new_expo / denom).astype(jnp.bfloat16)
    mixed = jnp.einsum('ht,td->hd', weights.astype(jnp.float32), values.astype(jnp.float32))
    mixed = mixed + new_weight.astype(jnp.float32)[:, None] * new_value.astype(jnp.float32)[None, :]
    return mixed.astype(jnp.bfloat16).reshape(HEADS * HEAD_DIM)

def reference(activations, ln_gain, w_query, w_keyval, w_out, k_cache, v_cache, cache_lengths):
    as_float = activations.astype(jnp.float32)
    row_mean = lax.optimization_barrier(jnp.sum(as_float, axis=1)) / D
    row_var = lax.optimization_barrier(jnp.sum(as_float * as_float, axis=1)) / D - row_mean * row_mean
    normed = ((as_float - row_mean[:, None]) * lax.rsqrt(row_var + 1e-06)[:, None] * ln_gain.astype(jnp.float32)).astype(jnp.bfloat16)
    queries = jnp.dot(normed, w_query, preferred_element_type=jnp.float32).astype(jnp.bfloat16)
    keyval = jnp.dot(normed, w_keyval, preferred_element_type=jnp.float32).astype(jnp.bfloat16)
    new_key = keyval[:, :HEAD_DIM]
    new_value = keyval[:, HEAD_DIM:]
    query_heads = queries.reshape(BATCH, HEADS, HEAD_DIM)
    attended = lax.map(attend_one, (query_heads, k_cache, v_cache, cache_lengths, new_key, new_value))
    return jnp.dot(attended, w_out, preferred_element_type=jnp.float32).astype(jnp.bfloat16)
```

```python
import jax
import jax.numpy as jnp
from jax import lax
from jax.sharding import PartitionSpec as P

D = 18432
WIRE_SCALE = 16.0


def swap(x, axis, n, m):
    return lax.ppermute(x, axis, [(k, k ^ m) for k in range(n)])


def rows_of(x, block, n):
    size = x.shape[0] // n
    return lax.dynamic_slice_in_dim(x, block * size, size, 0)


def reduce_rows(partial, axis, n, encode, decode):
    me = lax.axis_index(axis)
    got = [swap(encode(rows_of(partial, me ^ m, n)), axis, n, m) for m in range(1, n)]
    total = rows_of(partial, me, n)
    for part in got:
        total = total + decode(part)
    return total


def gather_rows(x, axis, n):
    me = lax.axis_index(axis)
    got = [x] + [swap(x, axis, n, m) for m in range(1, n)]
    out = jnp.zeros((n * x.shape[0],) + x.shape[1:], x.dtype)
    for m in range(n):
        out = lax.dynamic_update_slice_in_dim(out, got[m], (me ^ m) * x.shape[0], 0)
    return out


def attend_local(query_heads, new_key, new_value, k_cache, v_cache, cache_lengths):
    scores = (
        jnp.einsum("shd,std->sht", query_heads, k_cache, preferred_element_type=jnp.float32)
        * 0.0625
    )
    new_score = (
        jnp.einsum("shd,sd->sh", query_heads, new_key, preferred_element_type=jnp.float32) * 0.0625
    )
    positions = lax.broadcasted_iota(jnp.int32, (1, 1, k_cache.shape[1]), 2)
    live = positions < cache_lengths[:, None, None]
    masked = jnp.where(live, scores, jnp.float32(-1e30))
    top = jnp.maximum(jnp.max(masked, axis=2), new_score)
    expo = jnp.where(live, jnp.exp(masked - top[:, :, None]), jnp.float32(0.0))
    new_expo = jnp.exp(new_score - top)
    denom = jnp.sum(expo, axis=2) + new_expo
    weights = (expo / denom[:, :, None]).astype(jnp.bfloat16)
    new_weight = (new_expo / denom).astype(jnp.bfloat16)
    mixed = jnp.einsum("sht,std->shd", weights, v_cache, preferred_element_type=jnp.float32)
    mixed = (
        mixed
        + new_weight.astype(jnp.float32)[:, :, None] * new_value.astype(jnp.float32)[:, None, :]
    )
    return mixed.astype(jnp.bfloat16)


def make(nx, ny):
    def to_wire(x):
        return (x * WIRE_SCALE).astype(jnp.float16)

    def from_wire(x):
        return x.astype(jnp.float32) * (1.0 / WIRE_SCALE)

    def shards(activations, ln_gain, w_query, w_keyval, w_out, k_cache, v_cache, cache_lengths):
        gy = lax.axis_index("gy")
        head_dim = k_cache.shape[2]
        seqs = k_cache.shape[0]
        as_float = activations.astype(jnp.float32)
        sums = jnp.stack([jnp.sum(as_float, axis=1), jnp.sum(as_float * as_float, axis=1)])
        moments = sums
        for part in [swap(sums, "gx", nx, m) for m in range(1, nx)]:
            moments = moments + part
        row_mean = moments[0] / D
        row_var = moments[1] / D - row_mean * row_mean
        normed = (
            (as_float - row_mean[:, None])
            * lax.rsqrt(row_var + 1e-06)[:, None]
            * ln_gain.astype(jnp.float32)
        ).astype(jnp.bfloat16)
        gathered = lax.all_gather(normed, "gy", axis=0, tiled=True)
        kv_cols = w_keyval.shape[1] // ny
        w_own = lax.dynamic_slice_in_dim(w_keyval, gy * kv_cols, kv_cols, 1)
        q_cols = w_query.shape[1]
        kv_sum = jnp.dot(gathered, w_own, preferred_element_type=jnp.float32)
        q_sum = jnp.dot(gathered, w_query, preferred_element_type=jnp.float32)
        part = reduce_rows(
            jnp.concatenate([q_sum, kv_sum], axis=1), "gx", nx, to_wire, from_wire
        ).astype(jnp.bfloat16)
        mixed = lax.all_to_all(
            part.reshape(ny, seqs, q_cols + kv_cols), "gy", split_axis=0, concat_axis=0, tiled=True
        )
        queries = mixed[:, :, :q_cols].reshape(ny, seqs, -1, head_dim)
        queries = queries.transpose(1, 0, 2, 3).reshape(seqs, -1, head_dim)
        keyval = mixed[:, :, q_cols:].transpose(1, 0, 2).reshape(seqs, -1)
        attended = attend_local(
            queries, keyval[:, :head_dim], keyval[:, head_dim:], k_cache, v_cache, cache_lengths
        ).reshape(seqs, -1)
        returned = lax.all_to_all(attended, "gy", split_axis=1, concat_axis=0, tiled=True)
        everyone = gather_rows(returned, "gx", nx)
        partial_terms = jnp.dot(everyone, w_out, preferred_element_type=jnp.float32)
        return reduce_rows(
            partial_terms,
            "gy",
            ny,
            lambda x: x.astype(jnp.bfloat16),
            lambda x: x.astype(jnp.float32),
        ).astype(jnp.bfloat16)

    return shards


def solution(mesh):
    placed = (
        P(("groups", "gy"), "gx"),
        P("gx"),
        P("gx", "gy"),
        P("gx", None),
        P("gy", "gx"),
        P(("groups", "gx", "gy"), None, None),
        P(("groups", "gx", "gy"), None, None),
        P(("groups", "gx", "gy")),
    )
    return jax.shard_map(
        make(mesh.shape["gx"], mesh.shape["gy"]),
        mesh=mesh,
        in_specs=placed,
        out_specs=P(("groups", "gy"), "gx"),
        check_vma=False,
    )
```

```python
import jax
import jax.numpy as jnp
from jax import lax
from jax.sharding import PartitionSpec as P
import jax.experimental.pallas as pl
import jax.experimental.pallas.tpu as pltpu

D = 18432
WIRE_SCALE = 16.0


def swap(x, axis, n, m):
    return lax.ppermute(x, axis, [(k, k ^ m) for k in range(n)])


def rows_of(x, block, n):
    size = x.shape[0] // n
    return lax.dynamic_slice_in_dim(x, block * size, size, 0)


def far_first(n):
    return list(range(n // 2, n)) + list(range(1, n // 2))


def exchange(parts, axis, n):
    back = {m: swap(parts[m], axis, n, m) for m in far_first(n)}
    return [parts[0]] + [back[m] for m in range(1, n)]


def reduce_rows(partial, axis, n, encode, decode):
    me = lax.axis_index(axis)
    got = [swap(encode(rows_of(partial, me ^ m, n)), axis, n, m) for m in far_first(n)]
    total = rows_of(partial, me, n)
    for part in got:
        total = total + decode(part)
    return total


def in_order(parts, axis):
    me = lax.axis_index(axis)
    size = parts[0].shape[0]
    out = jnp.zeros((len(parts) * size,) + parts[0].shape[1:], parts[0].dtype)
    for m in [0] + far_first(len(parts)):
        out = lax.dynamic_update_slice_in_dim(out, parts[m], (me ^ m) * size, 0)
    return out


def gather_rows(x, axis, n):
    return in_order(exchange([x] * n, axis, n), axis)


def double_rows(x, axis, n):
    me = lax.axis_index(axis)
    size = x.shape[0]
    held = x[None]
    bit = n // 2
    while bit:
        other = swap(held, axis, n, bit)
        low = (me & bit) == 0
        held = jnp.stack([jnp.where(low, held, other), jnp.where(low, other, held)])
        held = held.reshape((-1,) + x.shape)
        bit //= 2
    bits = n.bit_length() - 1
    held = held.reshape((2,) * bits + x.shape)
    held = held.transpose(tuple(reversed(range(bits))) + (bits, bits + 1))
    return held.reshape(n * size, x.shape[1])


def in_vmem():
    return pl.BlockSpec(memory_space=pltpu.VMEM)


def dot_f32(x, w):
    return jnp.dot(x, w, preferred_element_type=jnp.float32)


def fetch(w, start, cols, after):
    def body(w_ref, after_ref, out_ref, sem):
        copy = pltpu.make_async_copy(w_ref.at[:, pl.ds(start, cols)], out_ref, sem)
        copy.start()
        copy.wait()

    rows = w.shape[0]
    return pl.pallas_call(
        body,
        out_shape=pltpu.VMEM((rows, cols), w.dtype),
        in_specs=[pl.BlockSpec(memory_space=pltpu.HBM), pl.BlockSpec(memory_space=pl.ANY)],
        out_specs=in_vmem(),
        scratch_shapes=[pltpu.SemaphoreType.DMA],
        compiler_params=pltpu.CompilerParams(vmem_limit_bytes=1 << 20),
        cost_estimate=pl.CostEstimate(
            flops=0, bytes_accessed=2 * rows * cols, transcendentals=0
        ),
        name="fetch",
    )(pltpu.with_memory_space_constraint(w, pltpu.HBM), after)


def tiles(cols, size=512):
    return [(c, min(size, cols - c)) for c in range(0, cols, size)]


def project(x, w_head, w_all, w_last, last_cols, axis):
    depth, cols = w_all.shape
    held = w_head.shape[1]
    rest = tiles(cols - held)
    whole_tiles = last_cols % 128 == 0
    if not whole_tiles:
        start = lax.axis_index(axis) * last_cols
        w_last = lax.dynamic_slice_in_dim(w_last, start, last_cols, 1)

    def body(x_ref, head_ref, all_ref, last_ref, out_ref, scratch, last_scratch, sems):
        start = 0
        if whole_tiles:
            start = pl.multiple_of(lax.axis_index(axis) * last_cols, 128)
        first = pltpu.make_async_copy(
            last_ref.at[:, pl.ds(start, last_cols)], last_scratch, sems.at[len(rest)]
        )
        copies = [
            pltpu.make_async_copy(
                all_ref.at[:, pl.ds(held + c, size)], scratch.at[:, pl.ds(c, size)], sems.at[i]
            )
            for i, (c, size) in enumerate(rest)
        ]
        for copy in [first] + copies:
            copy.start()
        for c, size in tiles(held):
            out_ref[:, c : c + size] = dot_f32(x_ref[...], head_ref[:, c : c + size])
        first.wait()
        out_ref[:, cols : cols + last_cols] = dot_f32(x_ref[...], last_scratch[...])
        for copy, (c, size) in zip(copies, rest):
            copy.wait()
            out_ref[:, held + c : held + c + size] = dot_f32(x_ref[...], scratch[:, c : c + size])

    rows = x.shape[0]
    in_hbm = pl.BlockSpec(memory_space=pltpu.HBM)
    return pl.pallas_call(
        body,
        out_shape=jax.ShapeDtypeStruct((rows, cols + last_cols), jnp.float32),
        in_specs=[in_vmem(), in_vmem(), in_hbm, in_hbm],
        out_specs=in_vmem(),
        scratch_shapes=[
            pltpu.VMEM((depth, cols - held), w_all.dtype),
            pltpu.VMEM((depth, last_cols), w_last.dtype),
            pltpu.SemaphoreType.DMA((len(rest) + 1,)),
        ],
        compiler_params=pltpu.CompilerParams(vmem_limit_bytes=28 << 20),
        cost_estimate=pl.CostEstimate(
            flops=2 * rows * depth * cols, bytes_accessed=2 * depth * cols, transcendentals=0
        ),
        name="project",
    )(
        x,
        pltpu.with_memory_space_constraint(w_head, pltpu.VMEM),
        pltpu.with_memory_space_constraint(w_all, pltpu.HBM),
        pltpu.with_memory_space_constraint(w_last, pltpu.HBM),
    )


def multiply_left(x, w_held, w_all, cut):
    depth, cols = w_all.shape
    held = w_held.shape[1]

    def body(x_ref, held_ref, all_ref, out_ref, rest_ref, sem):
        copy = pltpu.make_async_copy(all_ref.at[:, pl.ds(held, cols - held)], rest_ref, sem)
        copy.start()
        for c, size in tiles(cut):
            out_ref[:, c : c + size] = dot_f32(x_ref[...], held_ref[:, c : c + size])
        copy.wait()

    rows = x.shape[0]
    return pl.pallas_call(
        body,
        out_shape=[
            jax.ShapeDtypeStruct((rows, cut), jnp.float32),
            pltpu.VMEM((depth, cols - held), w_all.dtype),
        ],
        in_specs=[in_vmem(), in_vmem(), pl.BlockSpec(memory_space=pltpu.HBM)],
        out_specs=[in_vmem(), in_vmem()],
        scratch_shapes=[pltpu.SemaphoreType.DMA],
        compiler_params=pltpu.CompilerParams(vmem_limit_bytes=4 << 20),
        cost_estimate=pl.CostEstimate(
            flops=2 * rows * depth * cut, bytes_accessed=2 * depth * cut, transcendentals=0
        ),
        name="multiply_left",
    )(
        x,
        pltpu.with_memory_space_constraint(w_held, pltpu.VMEM),
        pltpu.with_memory_space_constraint(w_all, pltpu.HBM),
    )


def multiply_right(x, w_held, w_rest, cut):
    held, extra = w_held.shape[1] - cut, w_rest.shape[1]

    def body(x_ref, held_ref, rest_ref, out_ref):
        for c, size in tiles(held):
            out_ref[:, c : c + size] = dot_f32(x_ref[...], held_ref[:, cut + c : cut + c + size])
        for c, size in tiles(extra):
            out_ref[:, held + c : held + c + size] = dot_f32(x_ref[...], rest_ref[:, c : c + size])

    rows, depth = x.shape
    return pl.pallas_call(
        body,
        out_shape=jax.ShapeDtypeStruct((rows, held + extra), jnp.float32),
        in_specs=[in_vmem()] * 3,
        out_specs=in_vmem(),
        compiler_params=pltpu.CompilerParams(vmem_limit_bytes=4 << 20),
        cost_estimate=pl.CostEstimate(
            flops=2 * rows * depth * (held + extra),
            bytes_accessed=2 * depth * (held + extra),
            transcendentals=0,
        ),
        name="multiply_right",
    )(
        x,
        pltpu.with_memory_space_constraint(w_held, pltpu.VMEM),
        pltpu.with_memory_space_constraint(w_rest, pltpu.VMEM),
    )


def attend_local(query_heads, new_key, new_value, k_cache, v_cache, cache_lengths):
    scores = (
        jnp.einsum("shd,std->sht", query_heads, k_cache, preferred_element_type=jnp.float32)
        * 0.0625
    )
    new_score = (
        jnp.einsum("shd,sd->sh", query_heads, new_key, preferred_element_type=jnp.float32) * 0.0625
    )
    positions = lax.broadcasted_iota(jnp.int32, (1, 1, k_cache.shape[1]), 2)
    live = positions < cache_lengths[:, None, None]
    masked = jnp.where(live, scores, jnp.float32(-1e30))
    top = jnp.maximum(jnp.max(masked, axis=2), new_score)
    expo = jnp.where(live, jnp.exp(masked - top[:, :, None]), jnp.float32(0.0))
    new_expo = jnp.exp(new_score - top)
    denom = jnp.sum(expo, axis=2) + new_expo
    weights = (expo / denom[:, :, None]).astype(jnp.bfloat16)
    new_weight = (new_expo / denom).astype(jnp.bfloat16)
    mixed = jnp.einsum("sht,std->shd", weights, v_cache, preferred_element_type=jnp.float32)
    mixed = (
        mixed
        + new_weight.astype(jnp.float32)[:, :, None] * new_value.astype(jnp.float32)[:, None, :]
    )
    return mixed.astype(jnp.bfloat16)


def whole_tiles(cols):
    return cols // 128 * 128


def make(nx, ny):
    def to_wire(x):
        return (x * WIRE_SCALE).astype(jnp.float16)

    def from_wire(x):
        return x.astype(jnp.float32) * (1.0 / WIRE_SCALE)

    def shards(activations, ln_gain, w_query, w_keyval, w_out, k_cache, v_cache, cache_lengths):
        gy = lax.axis_index("gy")
        head_dim = k_cache.shape[2]
        seqs = k_cache.shape[0]
        own = activations.astype(jnp.float32)
        sums = jnp.stack([jnp.sum(own, axis=1), jnp.sum(own * own, axis=1)], axis=1)
        partial_moments = double_rows(sums, "gy", ny)
        moments = partial_moments
        as_float = double_rows(activations, "gy", ny).astype(jnp.float32)
        for part in exchange([moments] * nx, "gx", nx)[1:]:
            moments = moments + part
        row_mean = moments[:, 0] / D
        row_var = moments[:, 1] / D - row_mean * row_mean
        normed = (
            (as_float - row_mean[:, None])
            * lax.rsqrt(row_var + 1e-06)[:, None]
            * ln_gain.astype(jnp.float32)
        ).astype(jnp.bfloat16)
        kv_cols = w_keyval.shape[1] // ny
        q_cols = w_query.shape[1]
        w_head = fetch(w_query, 0, whole_tiles(q_cols * 3 // 8), partial_moments)
        projected = project(normed, w_head, w_query, w_keyval, kv_cols, "gy")
        part = reduce_rows(projected, "gx", nx, to_wire, from_wire).astype(jnp.bfloat16)
        mixed = exchange([rows_of(part, gy ^ m, ny) for m in range(ny)], "gy", ny)
        queries = jnp.concatenate(
            [x[:, :q_cols].reshape(seqs, -1, head_dim) for x in mixed], axis=1
        )
        keyval = in_order([x[:, q_cols:][None] for x in mixed], "gy")
        keyval = keyval.transpose(1, 0, 2).reshape(seqs, -1)
        attended = attend_local(
            queries, keyval[:, :head_dim], keyval[:, head_dim:], k_cache, v_cache, cache_lengths
        )
        heads = attended.shape[1] // ny
        returned = in_order(
            exchange(
                [attended[:, m * heads : (m + 1) * heads].reshape(seqs, -1) for m in range(ny)],
                "gy",
                ny,
            ),
            "gy",
        )
        width = w_out.shape[1]
        cut = whole_tiles(width * 5 // 8)
        w_held = fetch(w_out, 0, whole_tiles(width * 2 // 3), returned)
        everyone = gather_rows(returned, "gx", nx)
        left, w_rest = multiply_left(everyone, w_held, w_out, cut)
        right = multiply_right(everyone, w_held, w_rest, cut)
        outs = [
            reduce_rows(
                x,
                "gy",
                ny,
                lambda x: x.astype(jnp.bfloat16),
                lambda x: x.astype(jnp.float32),
            ).astype(jnp.bfloat16)
            for x in (left, right)
        ]
        return jnp.concatenate(outs, axis=1)

    return shards


def solution(mesh):
    placed = (
        P(("groups", "gy"), "gx"),
        P("gx"),
        P("gx", "gy"),
        P("gx", None),
        P("gy", "gx"),
        P(("groups", "gx", "gy"), None, None),
        P(("groups", "gx", "gy"), None, None),
        P(("groups", "gx", "gy")),
    )
    return jax.shard_map(
        make(mesh.shape["gx"], mesh.shape["gy"]),
        mesh=mesh,
        in_specs=placed,
        out_specs=P(("groups", "gy"), "gx"),
        check_vma=False,
    )
```

```python
import jax
import jax.numpy as jnp
from jax import lax
from jax.sharding import PartitionSpec as P
import jax.experimental.pallas as pl
import jax.experimental.pallas.tpu as pltpu

D = 18432
WIRE_SCALE = 16.0


def swap(x, axis, n, m):
    return lax.ppermute(x, axis, [(k, k ^ m) for k in range(n)])


def rows_of(x, block, n):
    size = x.shape[0] // n
    return lax.dynamic_slice_in_dim(x, block * size, size, 0)


def far_first(n):
    return list(range(n // 2, n)) + list(range(1, n // 2))


def exchange(parts, axis, n):
    back = {m: swap(parts[m], axis, n, m) for m in far_first(n)}
    return [parts[0]] + [back[m] for m in range(1, n)]


def reduce_rows(partial, axis, n, encode, decode):
    me = lax.axis_index(axis)
    got = [swap(encode(rows_of(partial, me ^ m, n)), axis, n, m) for m in far_first(n)]
    total = rows_of(partial, me, n)
    for part in got:
        total = total + decode(part)
    return total


def to_bfloat16(x):
    return x.astype(jnp.bfloat16)


def to_float32(x):
    return x.astype(jnp.float32)


def in_order(parts, axis):
    me = lax.axis_index(axis)
    size = parts[0].shape[0]
    out = jnp.zeros((len(parts) * size,) + parts[0].shape[1:], parts[0].dtype)
    for m in [0] + far_first(len(parts)):
        out = lax.dynamic_update_slice_in_dim(out, parts[m], (me ^ m) * size, 0)
    return out


def gather_rows(x, axis, n):
    return in_order(exchange([x] * n, axis, n), axis)


def double_rows(x, axis, n, steps):
    me = lax.axis_index(axis)
    size = x.shape[0]
    held = x[None]
    bit = n // 2
    while bit:
        other = swap(held, axis, n, bit)
        low = (me & bit) == 0
        held = jnp.stack([jnp.where(low, held, other), jnp.where(low, other, held)])
        held = held.reshape((-1,) + x.shape)
        steps.append(held)
        bit //= 2
    bits = n.bit_length() - 1
    held = held.reshape((2,) * bits + x.shape)
    held = held.transpose(tuple(reversed(range(bits))) + (bits, bits + 1))
    return held.reshape(n * size, x.shape[1])


def in_vmem():
    return pl.BlockSpec(memory_space=pltpu.VMEM)


def dot_f32(x, w):
    return jnp.dot(x, w, preferred_element_type=jnp.float32)


def row_sums(x):
    def body(x_ref, sums_ref, out_ref):
        value = x_ref[...]
        out_ref[...] = value
        value = value.astype(jnp.float32)
        sums_ref[:, 0:1] = jnp.sum(value, axis=1, keepdims=True)
        sums_ref[:, 1:2] = jnp.sum(value * value, axis=1, keepdims=True)

    return pl.pallas_call(
        body,
        out_shape=[
            jax.ShapeDtypeStruct((x.shape[0], 2), jnp.float32),
            jax.ShapeDtypeStruct(x.shape, x.dtype),
        ],
        in_specs=[in_vmem()],
        out_specs=[in_vmem()] * 2,
        compiler_params=pltpu.CompilerParams(vmem_limit_bytes=8 << 20),
        name="row_sums",
    )(x)


def fetch(w, start, cols, passed, *after):
    def body(w_ref, passed_ref, *refs):
        out_ref, passed_out, sem = refs[len(after) :]
        copy = pltpu.make_async_copy(w_ref.at[:, pl.ds(start, cols)], out_ref, sem)
        copy.start()
        passed_out[...] = passed_ref[...]
        copy.wait()

    rows = w.shape[0]
    return pl.pallas_call(
        body,
        out_shape=[
            pltpu.VMEM((rows, cols), w.dtype),
            pltpu.VMEM(passed.shape, passed.dtype),
        ],
        in_specs=[pl.BlockSpec(memory_space=pltpu.HBM), in_vmem()]
        + [pl.BlockSpec(memory_space=pl.ANY)] * len(after),
        out_specs=[in_vmem(), in_vmem()],
        scratch_shapes=[pltpu.SemaphoreType.DMA],
        compiler_params=pltpu.CompilerParams(vmem_limit_bytes=1 << 20),
        cost_estimate=pl.CostEstimate(
            flops=0, bytes_accessed=2 * rows * cols, transcendentals=0
        ),
        name="fetch",
    )(pltpu.with_memory_space_constraint(w, pltpu.HBM), passed, *after)


def tiles(cols, size=512):
    return [(c, min(size, cols - c)) for c in range(0, cols, size)]


def project(x, w_head, w_all, w_last, last_cols, axis):
    depth, cols = w_all.shape
    held = w_head.shape[1]
    rest = tiles(cols - held)
    whole_tiles = last_cols % 128 == 0
    if not whole_tiles:
        start = lax.axis_index(axis) * last_cols
        w_last = lax.dynamic_slice_in_dim(w_last, start, last_cols, 1)

    def body(x_ref, head_ref, all_ref, last_ref, out_ref, scratch, last_scratch, sems):
        start = 0
        if whole_tiles:
            start = pl.multiple_of(lax.axis_index(axis) * last_cols, 128)
        first = pltpu.make_async_copy(
            last_ref.at[:, pl.ds(start, last_cols)], last_scratch, sems.at[len(rest)]
        )
        copies = [
            pltpu.make_async_copy(
                all_ref.at[:, pl.ds(held + c, size)], scratch.at[:, pl.ds(c, size)], sems.at[i]
            )
            for i, (c, size) in enumerate(rest)
        ]
        for copy in [first] + copies:
            copy.start()
        for c, size in tiles(held):
            out_ref[:, c : c + size] = dot_f32(x_ref[...], head_ref[:, c : c + size])
        first.wait()
        out_ref[:, cols : cols + last_cols] = dot_f32(x_ref[...], last_scratch[...])
        for copy, (c, size) in zip(copies, rest):
            copy.wait()
            out_ref[:, held + c : held + c + size] = dot_f32(x_ref[...], scratch[:, c : c + size])

    rows = x.shape[0]
    in_hbm = pl.BlockSpec(memory_space=pltpu.HBM)
    return pl.pallas_call(
        body,
        out_shape=jax.ShapeDtypeStruct((rows, cols + last_cols), jnp.float32),
        in_specs=[in_vmem(), in_vmem(), in_hbm, in_hbm],
        out_specs=in_vmem(),
        scratch_shapes=[
            pltpu.VMEM((depth, cols - held), w_all.dtype),
            pltpu.VMEM((depth, last_cols), w_last.dtype),
            pltpu.SemaphoreType.DMA((len(rest) + 1,)),
        ],
        compiler_params=pltpu.CompilerParams(vmem_limit_bytes=28 << 20),
        cost_estimate=pl.CostEstimate(
            flops=2 * rows * depth * cols, bytes_accessed=2 * depth * cols, transcendentals=0
        ),
        name="project",
    )(
        x,
        pltpu.with_memory_space_constraint(w_head, pltpu.VMEM),
        pltpu.with_memory_space_constraint(w_all, pltpu.HBM),
        pltpu.with_memory_space_constraint(w_last, pltpu.HBM),
    )


def shares(total_ref, out_refs, axis, n):
    me = lax.axis_index(axis)
    rows = total_ref.shape[0] // n
    for m, out_ref in enumerate(out_refs):
        block = total_ref[pl.ds(pl.multiple_of((me ^ m) * rows, rows), rows), :]
        out_ref[...] = block.astype(out_ref.dtype)


def share_shapes(rows, cols, n):
    kept = jax.ShapeDtypeStruct((rows // n, cols), jnp.float32)
    return [kept] + [pltpu.VMEM((rows // n, cols), jnp.bfloat16)] * (n - 1)


def multiply_held(x, w, axis, n):
    rows, depth, cols = x.shape[0], x.shape[1], w.shape[1]

    def body(x_ref, w_ref, *refs):
        total = refs[-1]
        for c, size in tiles(cols):
            total[:, c : c + size] = dot_f32(x_ref[...], w_ref[:, c : c + size])
        shares(total, refs[:-1], axis, n)

    return pl.pallas_call(
        body,
        out_shape=share_shapes(rows, cols, n),
        in_specs=[in_vmem(), in_vmem()],
        out_specs=[in_vmem()] * n,
        scratch_shapes=[pltpu.VMEM((rows, cols), jnp.float32)],
        compiler_params=pltpu.CompilerParams(vmem_limit_bytes=8 << 20),
        cost_estimate=pl.CostEstimate(
            flops=2 * rows * depth * cols, bytes_accessed=2 * depth * cols, transcendentals=0
        ),
        name="multiply_held",
    )(x, pltpu.with_memory_space_constraint(w, pltpu.VMEM))


def multiply_streamed(x, w, start, axis, n):
    rows, depth = x.shape
    cols = w.shape[1] - start
    parts = tiles(cols, 384)

    def body(x_ref, w_ref, *refs):
        total, scratch, sems = refs[-3:]
        copies = [
            pltpu.make_async_copy(
                w_ref.at[:, pl.ds(start + c, size)], scratch.at[:, pl.ds(c, size)], sems.at[i]
            )
            for i, (c, size) in enumerate(parts)
        ]
        for copy in copies:
            copy.start()
        for copy, (c, size) in zip(copies, parts):
            copy.wait()
            total[:, c : c + size] = dot_f32(x_ref[...], scratch[:, c : c + size])
        shares(total, refs[:-3], axis, n)

    return pl.pallas_call(
        body,
        out_shape=share_shapes(rows, cols, n),
        in_specs=[in_vmem(), pl.BlockSpec(memory_space=pltpu.HBM)],
        out_specs=[in_vmem()] * n,
        scratch_shapes=[
            pltpu.VMEM((rows, cols), jnp.float32),
            pltpu.VMEM((depth, cols), w.dtype),
            pltpu.SemaphoreType.DMA((len(parts),)),
        ],
        compiler_params=pltpu.CompilerParams(vmem_limit_bytes=16 << 20),
        cost_estimate=pl.CostEstimate(
            flops=2 * rows * depth * cols, bytes_accessed=2 * depth * cols, transcendentals=0
        ),
        name="multiply_streamed",
    )(x, pltpu.with_memory_space_constraint(w, pltpu.HBM))


def attend_local(query_heads, new_key, new_value, k_cache, v_cache, cache_lengths):
    scores = (
        jnp.einsum("shd,std->sht", query_heads, k_cache, preferred_element_type=jnp.float32)
        * 0.0625
    )
    new_score = (
        jnp.einsum("shd,sd->sh", query_heads, new_key, preferred_element_type=jnp.float32) * 0.0625
    )
    positions = lax.broadcasted_iota(jnp.int32, (1, 1, k_cache.shape[1]), 2)
    live = positions < cache_lengths[:, None, None]
    masked = jnp.where(live, scores, jnp.float32(-1e30))
    top = jnp.maximum(jnp.max(masked, axis=2), new_score)
    expo = jnp.where(live, jnp.exp(masked - top[:, :, None]), jnp.float32(0.0))
    new_expo = jnp.exp(new_score - top)
    denom = jnp.sum(expo, axis=2) + new_expo
    weights = (expo / denom[:, :, None]).astype(jnp.bfloat16)
    new_weight = (new_expo / denom).astype(jnp.bfloat16)
    mixed = jnp.einsum("sht,std->shd", weights, v_cache, preferred_element_type=jnp.float32)
    mixed = (
        mixed
        + new_weight.astype(jnp.float32)[:, :, None] * new_value.astype(jnp.float32)[:, None, :]
    )
    return mixed.astype(jnp.bfloat16)


def whole_tiles(cols):
    return cols // 128 * 128


def make(nx, ny):
    def to_wire(x):
        return (x * WIRE_SCALE).astype(jnp.float16)

    def from_wire(x):
        return x.astype(jnp.float32) * (1.0 / WIRE_SCALE)

    def shards(activations, ln_gain, w_query, w_keyval, w_out, k_cache, v_cache, cache_lengths):
        gy = lax.axis_index("gy")
        head_dim = k_cache.shape[2]
        seqs = k_cache.shape[0]
        sums, own = row_sums(activations)
        partial_moments = double_rows(sums, "gy", ny, [])
        steps = []
        as_float = double_rows(own, "gy", ny, steps).astype(jnp.float32)
        q_cols = w_query.shape[1]
        w_head, moments = fetch(
            w_query, 0, whole_tiles(q_cols * 3 // 8), partial_moments, steps[0]
        )
        others, moments = lax.optimization_barrier(
            (exchange([partial_moments] * nx, "gx", nx)[1:], moments)
        )
        moments = sum(others, moments)
        row_mean = moments[:, 0] / D
        row_var = moments[:, 1] / D - row_mean * row_mean
        normed = (
            (as_float - row_mean[:, None])
            * lax.rsqrt(row_var + 1e-06)[:, None]
            * ln_gain.astype(jnp.float32)
        ).astype(jnp.bfloat16)
        kv_cols = w_keyval.shape[1] // ny
        projected = project(normed, w_head, w_query, w_keyval, kv_cols, "gy")
        part = reduce_rows(projected, "gx", nx, to_wire, from_wire).astype(jnp.bfloat16)
        mixed = exchange([rows_of(part, gy ^ m, ny) for m in range(ny)], "gy", ny)
        queries = jnp.concatenate(
            [x[:, :q_cols].reshape(seqs, -1, head_dim) for x in mixed], axis=1
        )
        keyval = in_order([x[:, q_cols:][None] for x in mixed], "gy")
        keyval = keyval.transpose(1, 0, 2).reshape(seqs, -1)
        attended = attend_local(
            queries, keyval[:, :head_dim], keyval[:, head_dim:], k_cache, v_cache, cache_lengths
        )
        heads = attended.shape[1] // ny
        returned = in_order(
            exchange(
                [attended[:, m * heads : (m + 1) * heads].reshape(seqs, -1) for m in range(ny)],
                "gy",
                ny,
            ),
            "gy",
        )
        cut = whole_tiles(w_out.shape[1] * 3 // 4)
        w_left, own = fetch(w_out, 0, cut, returned)
        everyone = in_order([own] + exchange([returned] * nx, "gx", nx)[1:], "gx")
        left = exchange(multiply_held(everyone, w_left, "gy", ny), "gy", ny)
        right = multiply_streamed(everyone, w_out, cut, "gy", ny)
        right, left[ny // 2] = lax.optimization_barrier((right, left[ny // 2]))
        right = exchange(right, "gy", ny)
        outs = [sum((to_float32(x) for x in parts[1:]), parts[0]) for parts in (left, right)]
        return jnp.concatenate([to_bfloat16(x) for x in outs], axis=1)

    return shards


def solution(mesh):
    placed = (
        P(("groups", "gy"), "gx"),
        P("gx"),
        P("gx", "gy"),
        P("gx", None),
        P("gy", "gx"),
        P(("groups", "gx", "gy"), None, None),
        P(("groups", "gx", "gy"), None, None),
        P(("groups", "gx", "gy")),
    )
    return jax.shard_map(
        make(mesh.shape["gx"], mesh.shape["gy"]),
        mesh=mesh,
        in_specs=placed,
        out_specs=P(("groups", "gy"), "gx"),
        check_vma=False,
    )
```

```python
import jax
import jax.numpy as jnp
from jax import lax
from jax.sharding import PartitionSpec as P
import jax.experimental.pallas as pl
import jax.experimental.pallas.tpu as pltpu

D = 18432
WIRE_SCALE = 16.0


def swap(x, axis, n, m):
    return lax.ppermute(x, axis, [(k, k ^ m) for k in range(n)])


def rows_of(x, block, n):
    size = x.shape[0] // n
    return lax.dynamic_slice_in_dim(x, block * size, size, 0)


def far_first(n):
    return list(range(n // 2, n)) + list(range(1, n // 2))


def order_of(n):
    return far_first(n)[::-1]


def exchange(parts, axis, n):
    back = {m: swap(parts[m], axis, n, m) for m in far_first(n)}
    return [parts[0]] + [back[m] for m in range(1, n)]


def to_bfloat16(x):
    return x.astype(jnp.bfloat16)


def to_float32(x):
    return x.astype(jnp.float32)


def in_order(parts, axis):
    me = lax.axis_index(axis)
    size = parts[0].shape[0]
    out = jnp.zeros((len(parts) * size,) + parts[0].shape[1:], parts[0].dtype)
    for m in [0] + far_first(len(parts)):
        out = lax.dynamic_update_slice_in_dim(out, parts[m], (me ^ m) * size, 0)
    return out


def gather_rows(x, axis, n):
    return in_order(exchange([x] * n, axis, n), axis)


def double_rows(x, axis, n, steps):
    me = lax.axis_index(axis)
    size = x.shape[0]
    held = x[None]
    bit = n // 2
    while bit:
        other = swap(held, axis, n, bit)
        low = (me & bit) == 0
        held = jnp.stack([jnp.where(low, held, other), jnp.where(low, other, held)])
        held = held.reshape((-1,) + x.shape)
        steps.append(held)
        bit //= 2
    bits = n.bit_length() - 1
    held = held.reshape((2,) * bits + x.shape)
    held = held.transpose(tuple(reversed(range(bits))) + (bits, bits + 1))
    return held.reshape(n * size, x.shape[1])


def in_vmem():
    return pl.BlockSpec(memory_space=pltpu.VMEM)


def dot_f32(x, w):
    return jnp.dot(x, w, preferred_element_type=jnp.float32)


def row_sums(x):
    def body(x_ref, sums_ref, out_ref):
        value = x_ref[...]
        out_ref[...] = value
        value = value.astype(jnp.float32)
        sums_ref[:, 0:1] = jnp.sum(value, axis=1, keepdims=True)
        sums_ref[:, 1:2] = jnp.sum(value * value, axis=1, keepdims=True)

    return pl.pallas_call(
        body,
        out_shape=[
            jax.ShapeDtypeStruct((x.shape[0], 2), jnp.float32),
            jax.ShapeDtypeStruct(x.shape, x.dtype),
        ],
        in_specs=[in_vmem()],
        out_specs=[in_vmem()] * 2,
        compiler_params=pltpu.CompilerParams(vmem_limit_bytes=8 << 20),
        name="row_sums",
    )(x)


def fetch(w, start, cols, passed, *after):
    def body(w_ref, passed_ref, *refs):
        out_ref, passed_out, sem = refs[len(after) :]
        copy = pltpu.make_async_copy(w_ref.at[:, pl.ds(start, cols)], out_ref, sem)
        copy.start()
        passed_out[...] = passed_ref[...]
        copy.wait()

    rows = w.shape[0]
    return pl.pallas_call(
        body,
        out_shape=[
            pltpu.VMEM((rows, cols), w.dtype),
            pltpu.VMEM(passed.shape, passed.dtype),
        ],
        in_specs=[pl.BlockSpec(memory_space=pltpu.HBM), in_vmem()]
        + [pl.BlockSpec(memory_space=pl.ANY)] * len(after),
        out_specs=[in_vmem(), in_vmem()],
        scratch_shapes=[pltpu.SemaphoreType.DMA],
        compiler_params=pltpu.CompilerParams(vmem_limit_bytes=1 << 20),
        cost_estimate=pl.CostEstimate(
            flops=0, bytes_accessed=2 * rows * cols, transcendentals=0
        ),
        name="fetch",
    )(pltpu.with_memory_space_constraint(w, pltpu.HBM), passed, *after)


def set_aside(w, start, passed):
    rows, cols = w.shape[0], w.shape[1] - start

    def body(w_ref, passed_ref, out_ref, passed_out, sem):
        copy = pltpu.make_async_copy(w_ref.at[:, pl.ds(start, cols)], out_ref, sem)
        copy.start()
        passed_out[...] = passed_ref[...]
        copy.wait()

    return pl.pallas_call(
        body,
        out_shape=[
            jax.ShapeDtypeStruct((rows, cols), w.dtype),
            pltpu.VMEM(passed.shape, passed.dtype),
        ],
        in_specs=[pl.BlockSpec(memory_space=pltpu.HBM), in_vmem()],
        out_specs=[pl.BlockSpec(memory_space=pl.ANY), in_vmem()],
        scratch_shapes=[pltpu.SemaphoreType.DMA],
        compiler_params=pltpu.CompilerParams(vmem_limit_bytes=4 << 20),
        cost_estimate=pl.CostEstimate(
            flops=0, bytes_accessed=4 * rows * cols, transcendentals=0
        ),
        name="set_aside",
    )(pltpu.with_memory_space_constraint(w, pltpu.HBM), passed)


def tiles(cols, size=512):
    return [(c, min(size, cols - c)) for c in range(0, cols, size)]


def project(x, w_head, w_all, w_last, last_cols, axis):
    depth, cols = w_all.shape
    held = w_head.shape[1]
    rest = tiles(cols - held)
    whole_tiles = last_cols % 128 == 0
    if not whole_tiles:
        start = lax.axis_index(axis) * last_cols
        w_last = lax.dynamic_slice_in_dim(w_last, start, last_cols, 1)

    def body(x_ref, head_ref, all_ref, last_ref, out_ref, scratch, last_scratch, sems):
        start = 0
        if whole_tiles:
            start = pl.multiple_of(lax.axis_index(axis) * last_cols, 128)
        first = pltpu.make_async_copy(
            last_ref.at[:, pl.ds(start, last_cols)], last_scratch, sems.at[len(rest)]
        )
        copies = [
            pltpu.make_async_copy(
                all_ref.at[:, pl.ds(held + c, size)], scratch.at[:, pl.ds(c, size)], sems.at[i]
            )
            for i, (c, size) in enumerate(rest)
        ]
        for copy in [first] + copies:
            copy.start()
        for c, size in tiles(held):
            out_ref[:, c : c + size] = dot_f32(x_ref[...], head_ref[:, c : c + size])
        first.wait()
        out_ref[:, cols : cols + last_cols] = dot_f32(x_ref[...], last_scratch[...])
        for copy, (c, size) in zip(copies, rest):
            copy.wait()
            out_ref[:, held + c : held + c + size] = dot_f32(x_ref[...], scratch[:, c : c + size])

    rows = x.shape[0]
    in_hbm = pl.BlockSpec(memory_space=pltpu.HBM)
    return pl.pallas_call(
        body,
        out_shape=jax.ShapeDtypeStruct((rows, cols + last_cols), jnp.float32),
        in_specs=[in_vmem(), in_vmem(), in_hbm, in_hbm],
        out_specs=in_vmem(),
        scratch_shapes=[
            pltpu.VMEM((depth, cols - held), w_all.dtype),
            pltpu.VMEM((depth, last_cols), w_last.dtype),
            pltpu.SemaphoreType.DMA((len(rest) + 1,)),
        ],
        compiler_params=pltpu.CompilerParams(vmem_limit_bytes=28 << 20),
        cost_estimate=pl.CostEstimate(
            flops=2 * rows * depth * cols, bytes_accessed=2 * depth * cols, transcendentals=0
        ),
        name="project",
    )(
        x,
        pltpu.with_memory_space_constraint(w_head, pltpu.VMEM),
        pltpu.with_memory_space_constraint(w_all, pltpu.HBM),
        pltpu.with_memory_space_constraint(w_last, pltpu.HBM),
    )


def shares(total_ref, out_refs, axis, n):
    me = lax.axis_index(axis)
    rows = total_ref.shape[0] // n
    for m, out_ref in enumerate(out_refs):
        block = total_ref[pl.ds(pl.multiple_of((me ^ m) * rows, rows), rows), :]
        out_ref[...] = block.astype(out_ref.dtype)


def share_shapes(rows, cols, n):
    kept = jax.ShapeDtypeStruct((rows // n, cols), jnp.float32)
    return [kept] + [pltpu.VMEM((rows // n, cols), jnp.bfloat16)] * (n - 1)


def multiply_held(x, w, axis, n):
    rows, depth, cols = x.shape[0], x.shape[1], w.shape[1]

    def body(x_ref, w_ref, *refs):
        total = refs[-1]
        for c, size in tiles(cols):
            total[:, c : c + size] = dot_f32(x_ref[...], w_ref[:, c : c + size])
        shares(total, refs[:-1], axis, n)

    return pl.pallas_call(
        body,
        out_shape=share_shapes(rows, cols, n),
        in_specs=[in_vmem(), in_vmem()],
        out_specs=[in_vmem()] * n,
        scratch_shapes=[pltpu.VMEM((rows, cols), jnp.float32)],
        compiler_params=pltpu.CompilerParams(vmem_limit_bytes=8 << 20),
        cost_estimate=pl.CostEstimate(
            flops=2 * rows * depth * cols, bytes_accessed=2 * depth * cols, transcendentals=0
        ),
        name="multiply_held",
    )(x, pltpu.with_memory_space_constraint(w, pltpu.VMEM))


def attend_local(query_heads, new_key, new_value, k_cache, v_cache, cache_lengths):
    scores = (
        jnp.einsum("shd,std->sht", query_heads, k_cache, preferred_element_type=jnp.float32)
        * 0.0625
    )
    new_score = (
        jnp.einsum("shd,sd->sh", query_heads, new_key, preferred_element_type=jnp.float32) * 0.0625
    )
    positions = lax.broadcasted_iota(jnp.int32, (1, 1, k_cache.shape[1]), 2)
    live = positions < cache_lengths[:, None, None]
    masked = jnp.where(live, scores, jnp.float32(-1e30))
    top = jnp.maximum(jnp.max(masked, axis=2), new_score)
    expo = jnp.where(live, jnp.exp(masked - top[:, :, None]), jnp.float32(0.0))
    new_expo = jnp.exp(new_score - top)
    denom = jnp.sum(expo, axis=2) + new_expo
    weights = (expo / denom[:, :, None]).astype(jnp.bfloat16)
    new_weight = (new_expo / denom).astype(jnp.bfloat16)
    mixed = jnp.einsum("sht,std->shd", weights, v_cache, preferred_element_type=jnp.float32)
    mixed = (
        mixed
        + new_weight.astype(jnp.float32)[:, :, None] * new_value.astype(jnp.float32)[:, None, :]
    )
    return mixed.astype(jnp.bfloat16)


def whole_tiles(cols):
    return cols // 128 * 128


def make(nx, ny):
    def to_wire(x):
        return (x * WIRE_SCALE).astype(jnp.float16)

    def from_wire(x):
        return x.astype(jnp.float32) * (1.0 / WIRE_SCALE)

    def shards(activations, ln_gain, w_query, w_keyval, w_out, k_cache, v_cache, cache_lengths):
        gy = lax.axis_index("gy")
        head_dim = k_cache.shape[2]
        seqs = k_cache.shape[0]
        sums, own = row_sums(activations)
        partial_moments = double_rows(sums, "gy", ny, [])
        steps = []
        as_float = double_rows(own, "gy", ny, steps).astype(jnp.float32)
        q_cols = w_query.shape[1]
        w_head, moments = fetch(
            w_query, 0, whole_tiles(q_cols * 3 // 8), partial_moments, steps[0]
        )
        others, moments = lax.optimization_barrier(
            (exchange([partial_moments] * nx, "gx", nx)[1:], moments)
        )
        moments = sum(others, moments)
        row_mean = moments[:, 0] / D
        row_var = moments[:, 1] / D - row_mean * row_mean
        normed = (
            (as_float - row_mean[:, None])
            * lax.rsqrt(row_var + 1e-06)[:, None]
            * ln_gain.astype(jnp.float32)
        ).astype(jnp.bfloat16)
        kv_cols = w_keyval.shape[1] // ny
        projected = project(normed, w_head, w_query, w_keyval, kv_cols, "gy")
        cut = whole_tiles(w_out.shape[1] * 11 // 16)
        me = lax.axis_index("gx")
        parts = [to_wire(rows_of(projected, me ^ m, nx)) for m in range(nx)]
        parts = exchange(parts, "gx", nx)[1:]
        w_right, part = set_aside(w_out, cut, rows_of(projected, me, nx))
        parts = [parts[m - 1] for m in order_of(nx)]
        parts, part = lax.optimization_barrier((parts, part))
        part = sum((from_wire(x) for x in parts), part).astype(jnp.bfloat16)
        mixed = exchange([rows_of(part, gy ^ m, ny) for m in range(ny)], "gy", ny)
        order = order_of(ny)
        arrived = lax.optimization_barrier([mixed[m] for m in order])
        mixed = mixed[:1] + [arrived[order.index(m)] for m in range(1, ny)]
        queries = jnp.concatenate(
            [x[:, :q_cols].reshape(seqs, -1, head_dim) for x in mixed], axis=1
        )
        keyval = in_order([x[:, q_cols:][None] for x in mixed], "gy")
        keyval = keyval.transpose(1, 0, 2).reshape(seqs, -1)
        attended = attend_local(
            queries, keyval[:, :head_dim], keyval[:, head_dim:], k_cache, v_cache, cache_lengths
        )
        heads = attended.shape[1] // ny
        returned = in_order(
            exchange(
                [attended[:, m * heads : (m + 1) * heads].reshape(seqs, -1) for m in range(ny)],
                "gy",
                ny,
            ),
            "gy",
        )
        w_left, own = fetch(w_out, 0, cut, returned)
        others = exchange([returned] * nx, "gx", nx)
        order = order_of(nx)
        arrived, own = lax.optimization_barrier(([others[m] for m in order], own))
        arrived = dict(zip(order, arrived))
        everyone = in_order([own] + [arrived[m] for m in range(1, nx)], "gx")
        left = exchange(multiply_held(everyone, w_left, "gy", ny), "gy", ny)
        right = multiply_held(everyone, w_right, "gy", ny)
        right, left[1] = lax.optimization_barrier((right, left[1]))
        right = exchange(right, "gy", ny)
        outs = [sum((to_float32(x) for x in parts[1:]), parts[0]) for parts in (left, right)]
        return jnp.concatenate([to_bfloat16(x) for x in outs], axis=1)

    return shards


def solution(mesh):
    placed = (
        P(("groups", "gy"), "gx"),
        P("gx"),
        P("gx", "gy"),
        P("gx", None),
        P("gy", "gx"),
        P(("groups", "gx", "gy"), None, None),
        P(("groups", "gx", "gy"), None, None),
        P(("groups", "gx", "gy")),
    )
    return jax.shard_map(
        make(mesh.shape["gx"], mesh.shape["gy"]),
        mesh=mesh,
        in_specs=placed,
        out_specs=P(("groups", "gy"), "gx"),
        check_vma=False,
    )
```

```python
import jax
import jax.numpy as jnp
from jax import lax
from jax.sharding import PartitionSpec as P
import jax.experimental.pallas as pl
import jax.experimental.pallas.tpu as pltpu

D = 18432


def swap(x, axis, n, m):
    return lax.ppermute(x, axis, [(k, k ^ m) for k in range(n)])


def rows_of(x, block, n):
    size = x.shape[0] // n
    return lax.dynamic_slice_in_dim(x, block * size, size, 0)


def far_first(n):
    return list(range(n // 2, n)) + list(range(1, n // 2))


def order_of(n):
    return far_first(n)


def exchange(parts, axis, n):
    back = {m: swap(parts[m], axis, n, m) for m in far_first(n)}
    return [parts[0]] + [back[m] for m in range(1, n)]


def in_order(parts, axis):
    me = lax.axis_index(axis)
    size = parts[0].shape[0]
    out = jnp.zeros((len(parts) * size,) + parts[0].shape[1:], parts[0].dtype)
    for m in [0] + far_first(len(parts)):
        out = lax.dynamic_update_slice_in_dim(out, parts[m], (me ^ m) * size, 0)
    return out


def gather_rows(x, axis, n):
    return in_order(exchange([x] * n, axis, n), axis)


def double_rows(x, axis, n, steps):
    me = lax.axis_index(axis)
    size = x.shape[0]
    held = x[None]
    bit = n // 2
    while bit:
        other = swap(held, axis, n, bit)
        low = (me & bit) == 0
        held = jnp.stack([jnp.where(low, held, other), jnp.where(low, other, held)])
        held = held.reshape((-1,) + x.shape)
        steps.append(held)
        bit //= 2
    bits = n.bit_length() - 1
    held = held.reshape((2,) * bits + x.shape)
    held = held.transpose(tuple(reversed(range(bits))) + (bits, bits + 1))
    return held.reshape(n * size, x.shape[1])


def in_vmem():
    return pl.BlockSpec(memory_space=pltpu.VMEM)


def dot_f32(x, w):
    return jnp.dot(x, w, preferred_element_type=jnp.float32)


def row_sums(x):
    def body(x_ref, sums_ref, out_ref):
        value = x_ref[...]
        out_ref[...] = value
        value = value.astype(jnp.float32)
        sums_ref[:, 0:1] = jnp.sum(value, axis=1, keepdims=True)
        sums_ref[:, 1:2] = jnp.sum(value * value, axis=1, keepdims=True)

    return pl.pallas_call(
        body,
        out_shape=[
            jax.ShapeDtypeStruct((x.shape[0], 2), jnp.float32),
            jax.ShapeDtypeStruct(x.shape, x.dtype),
        ],
        in_specs=[in_vmem()],
        out_specs=[in_vmem()] * 2,
        compiler_params=pltpu.CompilerParams(vmem_limit_bytes=8 << 20),
        name="row_sums",
    )(x)


def fetch(w, start, cols, passed, *after):
    def body(w_ref, passed_ref, *refs):
        out_ref, passed_out, sem = refs[len(after) :]
        copy = pltpu.make_async_copy(w_ref.at[:, pl.ds(start, cols)], out_ref, sem)
        copy.start()
        passed_out[...] = passed_ref[...]
        copy.wait()

    rows = w.shape[0]
    return pl.pallas_call(
        body,
        out_shape=[
            pltpu.VMEM((rows, cols), w.dtype),
            pltpu.VMEM(passed.shape, passed.dtype),
        ],
        in_specs=[pl.BlockSpec(memory_space=pltpu.HBM), in_vmem()]
        + [pl.BlockSpec(memory_space=pl.ANY)] * len(after),
        out_specs=[in_vmem(), in_vmem()],
        scratch_shapes=[pltpu.SemaphoreType.DMA],
        compiler_params=pltpu.CompilerParams(vmem_limit_bytes=1 << 20),
        cost_estimate=pl.CostEstimate(
            flops=0, bytes_accessed=2 * rows * cols, transcendentals=0
        ),
        name="fetch",
    )(pltpu.with_memory_space_constraint(w, pltpu.HBM), passed, *after)


def set_aside(w, start, passed):
    rows, cols = w.shape[0], w.shape[1] - start

    def body(w_ref, passed_ref, out_ref, passed_out, sem):
        copy = pltpu.make_async_copy(w_ref.at[:, pl.ds(start, cols)], out_ref, sem)
        copy.start()
        passed_out[...] = passed_ref[...]
        copy.wait()

    return pl.pallas_call(
        body,
        out_shape=[
            jax.ShapeDtypeStruct((rows, cols), w.dtype),
            pltpu.VMEM(passed.shape, passed.dtype),
        ],
        in_specs=[pl.BlockSpec(memory_space=pltpu.HBM), in_vmem()],
        out_specs=[pl.BlockSpec(memory_space=pl.ANY), in_vmem()],
        scratch_shapes=[pltpu.SemaphoreType.DMA],
        compiler_params=pltpu.CompilerParams(vmem_limit_bytes=4 << 20),
        cost_estimate=pl.CostEstimate(
            flops=0, bytes_accessed=4 * rows * cols, transcendentals=0
        ),
        name="set_aside",
    )(pltpu.with_memory_space_constraint(w, pltpu.HBM), passed)


def tiles(cols, size=512):
    return [(c, min(size, cols - c)) for c in range(0, cols, size)]


def padded(cols):
    return (cols + 127) // 128 * 128


def code(block):
    rows, cols = block.shape
    lane = lax.broadcasted_iota(jnp.int32, (rows, 128), 1)
    scales = jnp.zeros((rows, 128), jnp.int32)
    coded = []
    for g, (c, size) in enumerate(tiles(cols, 128)):
        part = block[:, c : c + size]
        top = jnp.maximum(jnp.max(jnp.abs(part), axis=1, keepdims=True), 1e-30)
        level = jnp.floor(16.0 * jnp.log2(32000.0 / top))
        coded.append(jnp.round(part * jnp.exp2(level * 0.0625)).astype(jnp.int32))
        scales = jnp.where(lane == g, level.astype(jnp.int32), scales)
        if size < 128:
            coded.append(jnp.zeros((rows, 128 - size), jnp.int32))
    return jnp.concatenate(coded + [scales], axis=1).astype(jnp.int16)


def combine(sums):
    rows = sums[0][0].shape[0]
    widths = [own.shape[1] for own, _ in sums]

    def body(*refs):
        refs, out_ref = list(refs[:-1]), refs[-1]
        at = 0
        for own, others in sums:
            own_ref = refs.pop(0)
            other_refs = [refs.pop(0) for _ in others]
            cols = own.shape[1]
            scales = [
                jnp.exp2(ref[:, padded(cols) :].astype(jnp.int32).astype(jnp.float32) * -0.0625)
                for ref in other_refs
            ]
            for g, (c, size) in enumerate(tiles(cols, 128)):
                total = own_ref[:, c : c + size]
                for ref, scale in zip(other_refs, scales):
                    value = ref[:, c : c + size].astype(jnp.int32).astype(jnp.float32)
                    total = total + value * scale[:, g : g + 1]
                out_ref[:, at + c : at + c + size] = total.astype(jnp.bfloat16)
            at += cols

    flat = [x for own, others in sums for x in [own, *others]]
    return pl.pallas_call(
        body,
        out_shape=jax.ShapeDtypeStruct((rows, sum(widths)), jnp.bfloat16),
        in_specs=[in_vmem()] * len(flat),
        out_specs=in_vmem(),
        compiler_params=pltpu.CompilerParams(vmem_limit_bytes=8 << 20),
        name="combine",
    )(*flat)


def shares(total_ref, out_refs, axis, n):
    me = lax.axis_index(axis)
    rows = total_ref.shape[0] // n
    for m, out_ref in enumerate(out_refs):
        block = total_ref[pl.ds(pl.multiple_of((me ^ m) * rows, rows), rows), :]
        out_ref[...] = code(block) if m else block


def share_shapes(rows, cols, n):
    kept = jax.ShapeDtypeStruct((rows // n, cols), jnp.float32)
    return [kept] + [pltpu.VMEM((rows // n, padded(cols) + 128), jnp.int16)] * (n - 1)


def project(x, w_head, w_all, w_last, last_cols, axis, share_axis, n):
    depth, cols = w_all.shape
    held = w_head.shape[1]
    rest = tiles(cols - held)
    whole_tiles = last_cols % 128 == 0
    if not whole_tiles:
        start = lax.axis_index(axis) * last_cols
        w_last = lax.dynamic_slice_in_dim(w_last, start, last_cols, 1)

    def body(x_ref, head_ref, all_ref, last_ref, *refs):
        out_ref, scratch, last_scratch, sems = refs[-4:]
        start = 0
        if whole_tiles:
            start = pl.multiple_of(lax.axis_index(axis) * last_cols, 128)
        first = pltpu.make_async_copy(
            last_ref.at[:, pl.ds(start, last_cols)], last_scratch, sems.at[len(rest)]
        )
        copies = [
            pltpu.make_async_copy(
                all_ref.at[:, pl.ds(held + c, size)], scratch.at[:, pl.ds(c, size)], sems.at[i]
            )
            for i, (c, size) in enumerate(rest)
        ]
        for copy in [first] + copies:
            copy.start()
        for c, size in tiles(held):
            out_ref[:, c : c + size] = dot_f32(x_ref[...], head_ref[:, c : c + size])
        first.wait()
        out_ref[:, cols : cols + last_cols] = dot_f32(x_ref[...], last_scratch[...])
        for copy, (c, size) in zip(copies, rest):
            copy.wait()
            out_ref[:, held + c : held + c + size] = dot_f32(x_ref[...], scratch[:, c : c + size])
        shares(out_ref, refs[:-4], share_axis, n)

    rows = x.shape[0]
    in_hbm = pl.BlockSpec(memory_space=pltpu.HBM)
    return pl.pallas_call(
        body,
        out_shape=share_shapes(rows, cols + last_cols, n),
        in_specs=[in_vmem(), in_vmem(), in_hbm, in_hbm],
        out_specs=[in_vmem()] * n,
        scratch_shapes=[
            pltpu.VMEM((rows, cols + last_cols), jnp.float32),
            pltpu.VMEM((depth, cols - held), w_all.dtype),
            pltpu.VMEM((depth, last_cols), w_last.dtype),
            pltpu.SemaphoreType.DMA((len(rest) + 1,)),
        ],
        compiler_params=pltpu.CompilerParams(vmem_limit_bytes=28 << 20),
        cost_estimate=pl.CostEstimate(
            flops=2 * rows * depth * cols, bytes_accessed=2 * depth * cols, transcendentals=0
        ),
        name="project",
    )(
        x,
        pltpu.with_memory_space_constraint(w_head, pltpu.VMEM),
        pltpu.with_memory_space_constraint(w_all, pltpu.HBM),
        pltpu.with_memory_space_constraint(w_last, pltpu.HBM),
    )


def multiply_held(x, w, axis, n):
    rows, depth, cols = x.shape[0], x.shape[1], w.shape[1]

    def body(x_ref, w_ref, *refs):
        total = refs[-1]
        for c, size in tiles(cols):
            total[:, c : c + size] = dot_f32(x_ref[...], w_ref[:, c : c + size])
        shares(total, refs[:-1], axis, n)

    return pl.pallas_call(
        body,
        out_shape=share_shapes(rows, cols, n),
        in_specs=[in_vmem(), in_vmem()],
        out_specs=[in_vmem()] * n,
        scratch_shapes=[pltpu.VMEM((rows, cols), jnp.float32)],
        compiler_params=pltpu.CompilerParams(vmem_limit_bytes=8 << 20),
        cost_estimate=pl.CostEstimate(
            flops=2 * rows * depth * cols, bytes_accessed=2 * depth * cols, transcendentals=0
        ),
        name="multiply_held",
    )(x, pltpu.with_memory_space_constraint(w, pltpu.VMEM))


def attend_local(query_heads, new_key, new_value, k_cache, v_cache, cache_lengths):
    scores = (
        jnp.einsum("shd,std->sht", query_heads, k_cache, preferred_element_type=jnp.float32)
        * 0.0625
    )
    new_score = (
        jnp.einsum("shd,sd->sh", query_heads, new_key, preferred_element_type=jnp.float32) * 0.0625
    )
    positions = lax.broadcasted_iota(jnp.int32, (1, 1, k_cache.shape[1]), 2)
    live = positions < cache_lengths[:, None, None]
    masked = jnp.where(live, scores, jnp.float32(-1e30))
    top = jnp.maximum(jnp.max(masked, axis=2), new_score)
    expo = jnp.where(live, jnp.exp(masked - top[:, :, None]), jnp.float32(0.0))
    new_expo = jnp.exp(new_score - top)
    denom = jnp.sum(expo, axis=2) + new_expo
    weights = (expo / denom[:, :, None]).astype(jnp.bfloat16)
    new_weight = (new_expo / denom).astype(jnp.bfloat16)
    mixed = jnp.einsum("sht,std->shd", weights, v_cache, preferred_element_type=jnp.float32)
    mixed = (
        mixed
        + new_weight.astype(jnp.float32)[:, :, None] * new_value.astype(jnp.float32)[:, None, :]
    )
    return mixed.astype(jnp.bfloat16)


def whole_tiles(cols):
    return cols // 128 * 128


def make(nx, ny):
    def shards(activations, ln_gain, w_query, w_keyval, w_out, k_cache, v_cache, cache_lengths):
        gy = lax.axis_index("gy")
        head_dim = k_cache.shape[2]
        seqs = k_cache.shape[0]
        sums, own = row_sums(activations)
        partial_moments = double_rows(sums, "gy", ny, [])
        steps = []
        as_float = double_rows(own, "gy", ny, steps).astype(jnp.float32)
        q_cols = w_query.shape[1]
        w_head, moments = fetch(
            w_query, 0, whole_tiles(q_cols * 3 // 8), partial_moments, steps[0]
        )
        others, moments = lax.optimization_barrier(
            (exchange([partial_moments] * nx, "gx", nx)[1:], moments)
        )
        moments = sum(others, moments)
        row_mean = moments[:, 0] / D
        row_var = moments[:, 1] / D - row_mean * row_mean
        normed = (
            (as_float - row_mean[:, None])
            * lax.rsqrt(row_var + 1e-06)[:, None]
            * ln_gain.astype(jnp.float32)
        ).astype(jnp.bfloat16)
        kv_cols = w_keyval.shape[1] // ny
        projected = project(normed, w_head, w_query, w_keyval, kv_cols, "gy", "gx", nx)
        cut = whole_tiles(w_out.shape[1] * 11 // 16)
        parts = exchange(projected, "gx", nx)[1:]
        w_right, part = set_aside(w_out, cut, projected[0])
        parts = [parts[m - 1] for m in order_of(nx)]
        parts, part = lax.optimization_barrier((parts, part))
        part = combine([(part, parts)])
        mixed = exchange([rows_of(part, gy ^ m, ny) for m in range(ny)], "gy", ny)
        order = order_of(ny)
        arrived = lax.optimization_barrier([mixed[m] for m in order])
        mixed = mixed[:1] + [arrived[order.index(m)] for m in range(1, ny)]
        queries = jnp.concatenate(
            [x[:, :q_cols].reshape(seqs, -1, head_dim) for x in mixed], axis=1
        )
        keyval = in_order([x[:, q_cols:][None] for x in mixed], "gy")
        keyval = keyval.transpose(1, 0, 2).reshape(seqs, -1)
        attended = attend_local(
            queries, keyval[:, :head_dim], keyval[:, head_dim:], k_cache, v_cache, cache_lengths
        )
        heads = attended.shape[1] // ny
        returned = in_order(
            exchange(
                [attended[:, m * heads : (m + 1) * heads].reshape(seqs, -1) for m in range(ny)],
                "gy",
                ny,
            ),
            "gy",
        )
        w_left, own = fetch(w_out, 0, cut, returned)
        others = exchange([returned] * nx, "gx", nx)
        order = order_of(nx)
        arrived, own = lax.optimization_barrier(([others[m] for m in order], own))
        arrived = dict(zip(order, arrived))
        everyone = in_order([own] + [arrived[m] for m in range(1, nx)], "gx")
        left = exchange(multiply_held(everyone, w_left, "gy", ny), "gy", ny)
        right = multiply_held(everyone, w_right, "gy", ny)
        right, left[1] = lax.optimization_barrier((right, left[1]))
        right = exchange(right, "gy", ny)
        return combine([(parts[0], parts[1:]) for parts in (left, right)])

    return shards


def solution(mesh):
    placed = (
        P(("groups", "gy"), "gx"),
        P("gx"),
        P("gx", "gy"),
        P("gx", None),
        P("gy", "gx"),
        P(("groups", "gx", "gy"), None, None),
        P(("groups", "gx", "gy"), None, None),
        P(("groups", "gx", "gy")),
    )
    return jax.shard_map(
        make(mesh.shape["gx"], mesh.shape["gy"]),
        mesh=mesh,
        in_specs=placed,
        out_specs=P(("groups", "gy"), "gx"),
        check_vma=False,
    )
```

```python
import jax
import jax.numpy as jnp
from jax import lax
from jax.sharding import PartitionSpec as P
import jax.experimental.pallas as pl
import jax.experimental.pallas.tpu as pltpu

D = 18432


def swap(x, axis, n, m):
    return lax.ppermute(x, axis, [(k, k ^ m) for k in range(n)])


def rows_of(x, block, n):
    size = x.shape[0] // n
    return lax.dynamic_slice_in_dim(x, block * size, size, 0)


def far_first(n):
    return list(range(n // 2, n)) + list(range(1, n // 2))


def order_of(n):
    return far_first(n)


def exchange(parts, axis, n):
    back = {m: swap(parts[m], axis, n, m) for m in far_first(n)}
    return [parts[0]] + [back[m] for m in range(1, n)]


def in_order(parts, axis):
    me = lax.axis_index(axis)
    size = parts[0].shape[0]
    out = jnp.zeros((len(parts) * size,) + parts[0].shape[1:], parts[0].dtype)
    for m in [0] + far_first(len(parts)):
        out = lax.dynamic_update_slice_in_dim(out, parts[m], (me ^ m) * size, 0)
    return out


def gather_rows(x, axis, n):
    return in_order(exchange([x] * n, axis, n), axis)


def double_rows(x, axis, n, steps):
    me = lax.axis_index(axis)
    size = x.shape[0]
    held = x[None]
    bit = n // 2
    while bit:
        other = swap(held, axis, n, bit)
        low = (me & bit) == 0
        held = jnp.stack([jnp.where(low, held, other), jnp.where(low, other, held)])
        held = held.reshape((-1,) + x.shape)
        steps.append(held)
        bit //= 2
    bits = n.bit_length() - 1
    held = held.reshape((2,) * bits + x.shape)
    held = held.transpose(tuple(reversed(range(bits))) + (bits, bits + 1))
    return held.reshape(n * size, x.shape[1])


def in_vmem():
    return pl.BlockSpec(memory_space=pltpu.VMEM)


def dot_f32(x, w):
    return jnp.dot(x, w, preferred_element_type=jnp.float32)


def row_sums(x):
    def body(x_ref, sums_ref, out_ref):
        value = x_ref[...]
        out_ref[...] = value
        value = value.astype(jnp.float32)
        sums_ref[:, 0:1] = jnp.sum(value, axis=1, keepdims=True)
        sums_ref[:, 1:2] = jnp.sum(value * value, axis=1, keepdims=True)

    return pl.pallas_call(
        body,
        out_shape=[
            jax.ShapeDtypeStruct((x.shape[0], 2), jnp.float32),
            jax.ShapeDtypeStruct(x.shape, x.dtype),
        ],
        in_specs=[in_vmem()],
        out_specs=[in_vmem()] * 2,
        compiler_params=pltpu.CompilerParams(vmem_limit_bytes=8 << 20),
        name="row_sums",
    )(x)


def fetch(w, start, cols, passed, *after):
    def body(w_ref, passed_ref, *refs):
        out_ref, passed_out, sem = refs[len(after) :]
        copy = pltpu.make_async_copy(w_ref.at[:, pl.ds(start, cols)], out_ref, sem)
        copy.start()
        passed_out[...] = passed_ref[...]
        copy.wait()

    rows = w.shape[0]
    return pl.pallas_call(
        body,
        out_shape=[
            pltpu.VMEM((rows, cols), w.dtype),
            pltpu.VMEM(passed.shape, passed.dtype),
        ],
        in_specs=[pl.BlockSpec(memory_space=pltpu.HBM), in_vmem()]
        + [pl.BlockSpec(memory_space=pl.ANY)] * len(after),
        out_specs=[in_vmem(), in_vmem()],
        scratch_shapes=[pltpu.SemaphoreType.DMA],
        compiler_params=pltpu.CompilerParams(vmem_limit_bytes=1 << 20),
        cost_estimate=pl.CostEstimate(
            flops=0, bytes_accessed=2 * rows * cols, transcendentals=0
        ),
        name="fetch",
    )(pltpu.with_memory_space_constraint(w, pltpu.HBM), passed, *after)


def set_aside(w, start, passed):
    rows, cols = w.shape[0], w.shape[1] - start

    def body(w_ref, passed_ref, out_ref, passed_out, sem):
        copy = pltpu.make_async_copy(w_ref.at[:, pl.ds(start, cols)], out_ref, sem)
        copy.start()
        passed_out[...] = passed_ref[...]
        copy.wait()

    return pl.pallas_call(
        body,
        out_shape=[
            jax.ShapeDtypeStruct((rows, cols), w.dtype),
            pltpu.VMEM(passed.shape, passed.dtype),
        ],
        in_specs=[pl.BlockSpec(memory_space=pltpu.HBM), in_vmem()],
        out_specs=[pl.BlockSpec(memory_space=pl.ANY), in_vmem()],
        scratch_shapes=[pltpu.SemaphoreType.DMA],
        compiler_params=pltpu.CompilerParams(vmem_limit_bytes=4 << 20),
        cost_estimate=pl.CostEstimate(
            flops=0, bytes_accessed=4 * rows * cols, transcendentals=0
        ),
        name="set_aside",
    )(pltpu.with_memory_space_constraint(w, pltpu.HBM), passed)


def tiles(cols, size=512):
    return [(c, min(size, cols - c)) for c in range(0, cols, size)]


def padded(cols):
    return (cols + 127) // 128 * 128


def code(block):
    rows, cols = block.shape
    lane = lax.broadcasted_iota(jnp.int32, (rows, 128), 1)
    scales = jnp.zeros((rows, 128), jnp.int32)
    coded = []
    for g, (c, size) in enumerate(tiles(cols, 128)):
        part = block[:, c : c + size]
        top = jnp.maximum(jnp.max(jnp.abs(part), axis=1, keepdims=True), 1e-30)
        level = jnp.floor(16.0 * jnp.log2(32000.0 / top))
        coded.append(jnp.round(part * jnp.exp2(level * 0.0625)).astype(jnp.int32))
        scales = jnp.where(lane == g, level.astype(jnp.int32), scales)
        if size < 128:
            coded.append(jnp.zeros((rows, 128 - size), jnp.int32))
    return jnp.concatenate(coded + [scales], axis=1).astype(jnp.int16)


def combine(sums):
    rows = sums[0][0].shape[0]
    widths = [own.shape[1] for own, _ in sums]

    def body(*refs):
        refs, out_ref = list(refs[:-1]), refs[-1]
        at = 0
        for own, others in sums:
            own_ref = refs.pop(0)
            other_refs = [refs.pop(0) for _ in others]
            cols = own.shape[1]
            if others[0].dtype == jnp.bfloat16:
                total = own_ref[...]
                for ref in other_refs:
                    total = total + ref[...].astype(jnp.float32)
                out_ref[:, at : at + cols] = total.astype(jnp.bfloat16)
                at += cols
                continue
            scales = [
                jnp.exp2(ref[:, padded(cols) :].astype(jnp.int32).astype(jnp.float32) * -0.0625)
                for ref in other_refs
            ]
            for g, (c, size) in enumerate(tiles(cols, 128)):
                total = own_ref[:, c : c + size]
                for ref, scale in zip(other_refs, scales):
                    value = ref[:, c : c + size].astype(jnp.int32).astype(jnp.float32)
                    total = total + value * scale[:, g : g + 1]
                out_ref[:, at + c : at + c + size] = total.astype(jnp.bfloat16)
            at += cols

    flat = [x for own, others in sums for x in [own, *others]]
    return pl.pallas_call(
        body,
        out_shape=jax.ShapeDtypeStruct((rows, sum(widths)), jnp.bfloat16),
        in_specs=[in_vmem()] * len(flat),
        out_specs=in_vmem(),
        compiler_params=pltpu.CompilerParams(vmem_limit_bytes=8 << 20),
        name="combine",
    )(*flat)


def shares(total_ref, out_refs, axis, n):
    me = lax.axis_index(axis)
    rows = total_ref.shape[0] // n
    for m, out_ref in enumerate(out_refs):
        block = total_ref[pl.ds(pl.multiple_of((me ^ m) * rows, rows), rows), :]
        if m:
            block = code(block) if out_ref.dtype == jnp.int16 else block.astype(out_ref.dtype)
        out_ref[...] = block


def share_shapes(rows, cols, n, coded):
    kept = jax.ShapeDtypeStruct((rows // n, cols), jnp.float32)
    sent = pltpu.VMEM((rows // n, cols), jnp.bfloat16)
    if coded:
        sent = pltpu.VMEM((rows // n, padded(cols) + 128), jnp.int16)
    return [kept] + [sent] * (n - 1)


def project(x, w_head, w_all, w_last, last_cols, axis, share_axis, n):
    depth, cols = w_all.shape
    held = w_head.shape[1]
    rest = tiles(cols - held)
    whole_tiles = last_cols % 128 == 0
    if not whole_tiles:
        start = lax.axis_index(axis) * last_cols
        w_last = lax.dynamic_slice_in_dim(w_last, start, last_cols, 1)

    def body(x_ref, head_ref, all_ref, last_ref, *refs):
        out_ref, scratch, last_scratch, sems = refs[-4:]
        start = 0
        if whole_tiles:
            start = pl.multiple_of(lax.axis_index(axis) * last_cols, 128)
        first = pltpu.make_async_copy(
            last_ref.at[:, pl.ds(start, last_cols)], last_scratch, sems.at[len(rest)]
        )
        copies = [
            pltpu.make_async_copy(
                all_ref.at[:, pl.ds(held + c, size)], scratch.at[:, pl.ds(c, size)], sems.at[i]
            )
            for i, (c, size) in enumerate(rest)
        ]
        for copy in [first] + copies:
            copy.start()
        for c, size in tiles(held):
            out_ref[:, c : c + size] = dot_f32(x_ref[...], head_ref[:, c : c + size])
        first.wait()
        out_ref[:, cols : cols + last_cols] = dot_f32(x_ref[...], last_scratch[...])
        for copy, (c, size) in zip(copies, rest):
            copy.wait()
            out_ref[:, held + c : held + c + size] = dot_f32(x_ref[...], scratch[:, c : c + size])
        shares(out_ref, refs[:-4], share_axis, n)

    rows = x.shape[0]
    in_hbm = pl.BlockSpec(memory_space=pltpu.HBM)
    return pl.pallas_call(
        body,
        out_shape=share_shapes(rows, cols + last_cols, n, True),
        in_specs=[in_vmem(), in_vmem(), in_hbm, in_hbm],
        out_specs=[in_vmem()] * n,
        scratch_shapes=[
            pltpu.VMEM((rows, cols + last_cols), jnp.float32),
            pltpu.VMEM((depth, cols - held), w_all.dtype),
            pltpu.VMEM((depth, last_cols), w_last.dtype),
            pltpu.SemaphoreType.DMA((len(rest) + 1,)),
        ],
        compiler_params=pltpu.CompilerParams(vmem_limit_bytes=28 << 20),
        cost_estimate=pl.CostEstimate(
            flops=2 * rows * depth * cols, bytes_accessed=2 * depth * cols, transcendentals=0
        ),
        name="project",
    )(
        x,
        pltpu.with_memory_space_constraint(w_head, pltpu.VMEM),
        pltpu.with_memory_space_constraint(w_all, pltpu.HBM),
        pltpu.with_memory_space_constraint(w_last, pltpu.HBM),
    )


def multiply_held(x, w, axis, n):
    rows, depth, cols = x.shape[0], x.shape[1], w.shape[1]

    def body(x_ref, w_ref, *refs):
        total = refs[-1]
        for c, size in tiles(cols):
            total[:, c : c + size] = dot_f32(x_ref[...], w_ref[:, c : c + size])
        shares(total, refs[:-1], axis, n)

    return pl.pallas_call(
        body,
        out_shape=share_shapes(rows, cols, n, False),
        in_specs=[in_vmem(), in_vmem()],
        out_specs=[in_vmem()] * n,
        scratch_shapes=[pltpu.VMEM((rows, cols), jnp.float32)],
        compiler_params=pltpu.CompilerParams(vmem_limit_bytes=8 << 20),
        cost_estimate=pl.CostEstimate(
            flops=2 * rows * depth * cols, bytes_accessed=2 * depth * cols, transcendentals=0
        ),
        name="multiply_held",
    )(x, pltpu.with_memory_space_constraint(w, pltpu.VMEM))


def attend_local(query_heads, new_key, new_value, k_cache, v_cache, cache_lengths):
    scores = (
        jnp.einsum("shd,std->sht", query_heads, k_cache, preferred_element_type=jnp.float32)
        * 0.0625
    )
    new_score = (
        jnp.einsum("shd,sd->sh", query_heads, new_key, preferred_element_type=jnp.float32) * 0.0625
    )
    positions = lax.broadcasted_iota(jnp.int32, (1, 1, k_cache.shape[1]), 2)
    live = positions < cache_lengths[:, None, None]
    masked = jnp.where(live, scores, jnp.float32(-1e30))
    top = jnp.maximum(jnp.max(masked, axis=2), new_score)
    expo = jnp.where(live, jnp.exp(masked - top[:, :, None]), jnp.float32(0.0))
    new_expo = jnp.exp(new_score - top)
    denom = jnp.sum(expo, axis=2) + new_expo
    weights = (expo / denom[:, :, None]).astype(jnp.bfloat16)
    new_weight = (new_expo / denom).astype(jnp.bfloat16)
    mixed = jnp.einsum("sht,std->shd", weights, v_cache, preferred_element_type=jnp.float32)
    mixed = (
        mixed
        + new_weight.astype(jnp.float32)[:, :, None] * new_value.astype(jnp.float32)[:, None, :]
    )
    return mixed.astype(jnp.bfloat16)


def whole_tiles(cols):
    return cols // 128 * 128


def make(nx, ny):
    def shards(activations, ln_gain, w_query, w_keyval, w_out, k_cache, v_cache, cache_lengths):
        gy = lax.axis_index("gy")
        head_dim = k_cache.shape[2]
        seqs = k_cache.shape[0]
        sums, own = row_sums(activations)
        partial_moments = double_rows(sums, "gy", ny, [])
        steps = []
        as_float = double_rows(own, "gy", ny, steps).astype(jnp.float32)
        q_cols = w_query.shape[1]
        w_head, moments = fetch(
            w_query, 0, whole_tiles(q_cols * 3 // 8), partial_moments, steps[0]
        )
        others, moments = lax.optimization_barrier(
            (exchange([partial_moments] * nx, "gx", nx)[1:], moments)
        )
        moments = sum(others, moments)
        row_mean = moments[:, 0] / D
        row_var = moments[:, 1] / D - row_mean * row_mean
        normed = (
            (as_float - row_mean[:, None])
            * lax.rsqrt(row_var + 1e-06)[:, None]
            * ln_gain.astype(jnp.float32)
        ).astype(jnp.bfloat16)
        kv_cols = w_keyval.shape[1] // ny
        projected = project(normed, w_head, w_query, w_keyval, kv_cols, "gy", "gx", nx)
        cut = whole_tiles(w_out.shape[1] * 11 // 16)
        parts = exchange(projected, "gx", nx)[1:]
        w_right, part = set_aside(w_out, cut, projected[0])
        parts = [parts[m - 1] for m in order_of(nx)]
        parts, part = lax.optimization_barrier((parts, part))
        part = combine([(part, parts)])
        mixed = exchange([rows_of(part, gy ^ m, ny) for m in range(ny)], "gy", ny)
        order = order_of(ny)
        arrived = lax.optimization_barrier([mixed[m] for m in order])
        mixed = mixed[:1] + [arrived[order.index(m)] for m in range(1, ny)]
        queries = jnp.concatenate(
            [x[:, :q_cols].reshape(seqs, -1, head_dim) for x in mixed], axis=1
        )
        keyval = in_order([x[:, q_cols:][None] for x in mixed], "gy")
        keyval = keyval.transpose(1, 0, 2).reshape(seqs, -1)
        attended = attend_local(
            queries, keyval[:, :head_dim], keyval[:, head_dim:], k_cache, v_cache, cache_lengths
        )
        heads = attended.shape[1] // ny
        returned = in_order(
            exchange(
                [attended[:, m * heads : (m + 1) * heads].reshape(seqs, -1) for m in range(ny)],
                "gy",
                ny,
            ),
            "gy",
        )
        w_left, own = fetch(w_out, 0, cut, returned)
        others = exchange([returned] * nx, "gx", nx)
        order = order_of(nx)
        arrived, own = lax.optimization_barrier(([others[m] for m in order], own))
        arrived = dict(zip(order, arrived))
        everyone = in_order([own] + [arrived[m] for m in range(1, nx)], "gx")
        left = exchange(multiply_held(everyone, w_left, "gy", ny), "gy", ny)
        right = multiply_held(everyone, w_right, "gy", ny)
        right, left[1] = lax.optimization_barrier((right, left[1]))
        right = exchange(right, "gy", ny)
        return combine([(parts[0], parts[1:]) for parts in (left, right)])

    return shards


def solution(mesh):
    placed = (
        P(("groups", "gy"), "gx"),
        P("gx"),
        P("gx", "gy"),
        P("gx", None),
        P("gy", "gx"),
        P(("groups", "gx", "gy"), None, None),
        P(("groups", "gx", "gy"), None, None),
        P(("groups", "gx", "gy")),
    )
    return jax.shard_map(
        make(mesh.shape["gx"], mesh.shape["gy"]),
        mesh=mesh,
        in_specs=placed,
        out_specs=P(("groups", "gy"), "gx"),
        check_vma=False,
    )
```

```python
import jax
import jax.numpy as jnp
from jax import lax
from jax.sharding import PartitionSpec as P
import jax.experimental.pallas as pl
import jax.experimental.pallas.tpu as pltpu

D = 18432


def swap(x, axis, n, m):
    return lax.ppermute(x, axis, [(k, k ^ m) for k in range(n)])


def rows_of(x, block, n):
    size = x.shape[0] // n
    return lax.dynamic_slice_in_dim(x, block * size, size, 0)


def far_first(n):
    return list(range(n // 2, n)) + list(range(1, n // 2))


def order_of(n):
    return far_first(n)


def exchange(parts, axis, n):
    back = {m: swap(parts[m], axis, n, m) for m in far_first(n)}
    return [parts[0]] + [back[m] for m in range(1, n)]


def in_order(parts, axis):
    me = lax.axis_index(axis)
    size = parts[0].shape[0]
    out = jnp.zeros((len(parts) * size,) + parts[0].shape[1:], parts[0].dtype)
    for m in [0] + far_first(len(parts)):
        out = lax.dynamic_update_slice_in_dim(out, parts[m], (me ^ m) * size, 0)
    return out


def gather_rows(x, axis, n):
    return in_order(exchange([x] * n, axis, n), axis)


def double_rows(x, axis, n, steps):
    me = lax.axis_index(axis)
    size = x.shape[0]
    held = x[None]
    bit = n // 2
    while bit:
        other = swap(held, axis, n, bit)
        low = (me & bit) == 0
        held = jnp.stack([jnp.where(low, held, other), jnp.where(low, other, held)])
        held = held.reshape((-1,) + x.shape)
        steps.append(held)
        bit //= 2
    bits = n.bit_length() - 1
    held = held.reshape((2,) * bits + x.shape)
    held = held.transpose(tuple(reversed(range(bits))) + (bits, bits + 1))
    return held.reshape(n * size, x.shape[1])


def in_vmem():
    return pl.BlockSpec(memory_space=pltpu.VMEM)


def dot_f32(x, w):
    return jnp.dot(x, w, preferred_element_type=jnp.float32)


def row_sums(x):
    def body(x_ref, sums_ref, out_ref):
        value = x_ref[...]
        out_ref[...] = value
        value = value.astype(jnp.float32)
        sums_ref[:, 0:1] = jnp.sum(value, axis=1, keepdims=True)
        sums_ref[:, 1:2] = jnp.sum(value * value, axis=1, keepdims=True)

    return pl.pallas_call(
        body,
        out_shape=[
            jax.ShapeDtypeStruct((x.shape[0], 2), jnp.float32),
            jax.ShapeDtypeStruct(x.shape, x.dtype),
        ],
        in_specs=[in_vmem()],
        out_specs=[in_vmem()] * 2,
        compiler_params=pltpu.CompilerParams(vmem_limit_bytes=8 << 20),
        name="row_sums",
    )(x)


def fetch(w, start, cols, passed, *after):
    def body(w_ref, passed_ref, *refs):
        out_ref, passed_out, sem = refs[len(after) :]
        copy = pltpu.make_async_copy(w_ref.at[:, pl.ds(start, cols)], out_ref, sem)
        copy.start()
        passed_out[...] = passed_ref[...]
        copy.wait()

    rows = w.shape[0]
    return pl.pallas_call(
        body,
        out_shape=[
            pltpu.VMEM((rows, cols), w.dtype),
            pltpu.VMEM(passed.shape, passed.dtype),
        ],
        in_specs=[pl.BlockSpec(memory_space=pltpu.HBM), in_vmem()]
        + [pl.BlockSpec(memory_space=pl.ANY)] * len(after),
        out_specs=[in_vmem(), in_vmem()],
        scratch_shapes=[pltpu.SemaphoreType.DMA],
        compiler_params=pltpu.CompilerParams(vmem_limit_bytes=1 << 20),
        cost_estimate=pl.CostEstimate(
            flops=0, bytes_accessed=2 * rows * cols, transcendentals=0
        ),
        name="fetch",
    )(pltpu.with_memory_space_constraint(w, pltpu.HBM), passed, *after)


def set_aside(w, start, passed):
    rows, cols = w.shape[0], w.shape[1] - start

    def body(w_ref, passed_ref, out_ref, passed_out, sem):
        copy = pltpu.make_async_copy(w_ref.at[:, pl.ds(start, cols)], out_ref, sem)
        copy.start()
        passed_out[...] = passed_ref[...]
        copy.wait()

    return pl.pallas_call(
        body,
        out_shape=[
            jax.ShapeDtypeStruct((rows, cols), w.dtype),
            pltpu.VMEM(passed.shape, passed.dtype),
        ],
        in_specs=[pl.BlockSpec(memory_space=pltpu.HBM), in_vmem()],
        out_specs=[pl.BlockSpec(memory_space=pl.ANY), in_vmem()],
        scratch_shapes=[pltpu.SemaphoreType.DMA],
        compiler_params=pltpu.CompilerParams(vmem_limit_bytes=4 << 20),
        cost_estimate=pl.CostEstimate(
            flops=0, bytes_accessed=4 * rows * cols, transcendentals=0
        ),
        name="set_aside",
    )(pltpu.with_memory_space_constraint(w, pltpu.HBM), passed)


def tiles(cols, size=512):
    return [(c, min(size, cols - c)) for c in range(0, cols, size)]


def padded(cols):
    return (cols + 127) // 128 * 128


def code(block):
    rows, cols = block.shape
    lane = lax.broadcasted_iota(jnp.int32, (rows, 128), 1)
    scales = jnp.zeros((rows, 128), jnp.int32)
    coded = []
    for g, (c, size) in enumerate(tiles(cols, 128)):
        part = block[:, c : c + size]
        top = jnp.maximum(jnp.max(jnp.abs(part), axis=1, keepdims=True), 1e-30)
        level = jnp.floor(16.0 * jnp.log2(32000.0 / top))
        coded.append(jnp.round(part * jnp.exp2(level * 0.0625)).astype(jnp.int32))
        scales = jnp.where(lane == g, level.astype(jnp.int32), scales)
        if size < 128:
            coded.append(jnp.zeros((rows, 128 - size), jnp.int32))
    return jnp.concatenate(coded + [scales], axis=1).astype(jnp.int16)


def combine(sums):
    rows = sums[0][0].shape[0]
    widths = [own.shape[1] for own, _ in sums]

    def body(*refs):
        refs, out_ref = list(refs[:-1]), refs[-1]
        at = 0
        for own, others in sums:
            own_ref = refs.pop(0)
            other_refs = [refs.pop(0) for _ in others]
            cols = own.shape[1]
            if others[0].dtype == jnp.bfloat16:
                total = own_ref[...]
                for ref in other_refs:
                    total = total + ref[...].astype(jnp.float32)
                out_ref[:, at : at + cols] = total.astype(jnp.bfloat16)
                at += cols
                continue
            scales = [
                jnp.exp2(ref[:, padded(cols) :].astype(jnp.int32).astype(jnp.float32) * -0.0625)
                for ref in other_refs
            ]
            for g, (c, size) in enumerate(tiles(cols, 128)):
                total = own_ref[:, c : c + size]
                for ref, scale in zip(other_refs, scales):
                    value = ref[:, c : c + size].astype(jnp.int32).astype(jnp.float32)
                    total = total + value * scale[:, g : g + 1]
                out_ref[:, at + c : at + c + size] = total.astype(jnp.bfloat16)
            at += cols

    flat = [x for own, others in sums for x in [own, *others]]
    return pl.pallas_call(
        body,
        out_shape=jax.ShapeDtypeStruct((rows, sum(widths)), jnp.bfloat16),
        in_specs=[in_vmem()] * len(flat),
        out_specs=in_vmem(),
        compiler_params=pltpu.CompilerParams(vmem_limit_bytes=8 << 20),
        name="combine",
    )(*flat)


def shares(total_ref, out_refs, axis, n):
    me = lax.axis_index(axis)
    rows = total_ref.shape[0] // n
    for m, out_ref in enumerate(out_refs):
        block = total_ref[pl.ds(pl.multiple_of((me ^ m) * rows, rows), rows), :]
        if m:
            block = code(block) if out_ref.dtype == jnp.int16 else block.astype(out_ref.dtype)
        out_ref[...] = block


def share_shapes(rows, cols, n, coded):
    kept = jax.ShapeDtypeStruct((rows // n, cols), jnp.float32)
    sent = pltpu.VMEM((rows // n, cols), jnp.bfloat16)
    if coded:
        sent = pltpu.VMEM((rows // n, padded(cols) + 128), jnp.int16)
    return [kept] + [sent] * (n - 1)


def project(x, w_head, w_all, w_last, last_cols, axis, share_axis, n):
    depth, cols = w_all.shape
    held = w_head.shape[1]
    rest = tiles(cols - held)
    whole_tiles = last_cols % 128 == 0
    if not whole_tiles:
        start = lax.axis_index(axis) * last_cols
        w_last = lax.dynamic_slice_in_dim(w_last, start, last_cols, 1)

    def body(x_ref, head_ref, all_ref, last_ref, *refs):
        out_ref, scratch, last_scratch, sems = refs[-4:]
        start = 0
        if whole_tiles:
            start = pl.multiple_of(lax.axis_index(axis) * last_cols, 128)
        first = pltpu.make_async_copy(
            last_ref.at[:, pl.ds(start, last_cols)], last_scratch, sems.at[len(rest)]
        )
        copies = [
            pltpu.make_async_copy(
                all_ref.at[:, pl.ds(held + c, size)], scratch.at[:, pl.ds(c, size)], sems.at[i]
            )
            for i, (c, size) in enumerate(rest)
        ]
        for copy in [first] + copies:
            copy.start()
        for c, size in tiles(held):
            out_ref[:, c : c + size] = dot_f32(x_ref[...], head_ref[:, c : c + size])
        first.wait()
        out_ref[:, cols : cols + last_cols] = dot_f32(x_ref[...], last_scratch[...])
        for copy, (c, size) in zip(copies, rest):
            copy.wait()
            out_ref[:, held + c : held + c + size] = dot_f32(x_ref[...], scratch[:, c : c + size])
        shares(out_ref, refs[:-4], share_axis, n)

    rows = x.shape[0]
    in_hbm = pl.BlockSpec(memory_space=pltpu.HBM)
    return pl.pallas_call(
        body,
        out_shape=share_shapes(rows, cols + last_cols, n, True),
        in_specs=[in_vmem(), in_vmem(), in_hbm, in_hbm],
        out_specs=[in_vmem()] * n,
        scratch_shapes=[
            pltpu.VMEM((rows, cols + last_cols), jnp.float32),
            pltpu.VMEM((depth, cols - held), w_all.dtype),
            pltpu.VMEM((depth, last_cols), w_last.dtype),
            pltpu.SemaphoreType.DMA((len(rest) + 1,)),
        ],
        compiler_params=pltpu.CompilerParams(vmem_limit_bytes=28 << 20),
        cost_estimate=pl.CostEstimate(
            flops=2 * rows * depth * cols, bytes_accessed=2 * depth * cols, transcendentals=0
        ),
        name="project",
    )(
        x,
        pltpu.with_memory_space_constraint(w_head, pltpu.VMEM),
        pltpu.with_memory_space_constraint(w_all, pltpu.HBM),
        pltpu.with_memory_space_constraint(w_last, pltpu.HBM),
    )


def multiply_held(x, w, axis, n):
    rows, depth, cols = x.shape[0], x.shape[1], w.shape[1]

    def body(x_ref, w_ref, *refs):
        total = refs[-1]
        for c, size in tiles(cols):
            total[:, c : c + size] = dot_f32(x_ref[...], w_ref[:, c : c + size])
        shares(total, refs[:-1], axis, n)

    return pl.pallas_call(
        body,
        out_shape=share_shapes(rows, cols, n, False),
        in_specs=[in_vmem(), in_vmem()],
        out_specs=[in_vmem()] * n,
        scratch_shapes=[pltpu.VMEM((rows, cols), jnp.float32)],
        compiler_params=pltpu.CompilerParams(vmem_limit_bytes=8 << 20),
        cost_estimate=pl.CostEstimate(
            flops=2 * rows * depth * cols, bytes_accessed=2 * depth * cols, transcendentals=0
        ),
        name="multiply_held",
    )(x, pltpu.with_memory_space_constraint(w, pltpu.VMEM))


def attend_local(query_heads, new_key, new_value, k_cache, v_cache, cache_lengths):
    scores = (
        jnp.einsum("shd,std->sht", query_heads, k_cache, preferred_element_type=jnp.float32)
        * 0.0625
    )
    new_score = (
        jnp.einsum("shd,sd->sh", query_heads, new_key, preferred_element_type=jnp.float32) * 0.0625
    )
    positions = lax.broadcasted_iota(jnp.int32, (1, 1, k_cache.shape[1]), 2)
    live = positions < cache_lengths[:, None, None]
    masked = jnp.where(live, scores, jnp.float32(-1e30))
    top = jnp.maximum(jnp.max(masked, axis=2), new_score)
    expo = jnp.where(live, jnp.exp(masked - top[:, :, None]), jnp.float32(0.0))
    new_expo = jnp.exp(new_score - top)
    denom = jnp.sum(expo, axis=2) + new_expo
    weights = (expo / denom[:, :, None]).astype(jnp.bfloat16)
    new_weight = (new_expo / denom).astype(jnp.bfloat16)
    mixed = jnp.einsum("sht,std->shd", weights, v_cache, preferred_element_type=jnp.float32)
    mixed = (
        mixed
        + new_weight.astype(jnp.float32)[:, :, None] * new_value.astype(jnp.float32)[:, None, :]
    )
    return mixed.astype(jnp.bfloat16)


def whole_tiles(cols):
    return cols // 128 * 128


def make(nx, ny):
    def shards(activations, ln_gain, w_query, w_keyval, w_out, k_cache, v_cache, cache_lengths):
        gy = lax.axis_index("gy")
        head_dim = k_cache.shape[2]
        seqs = k_cache.shape[0]
        sums, own = row_sums(activations)
        partial_moments = double_rows(sums, "gy", ny, [])
        steps = []
        as_float = double_rows(own, "gy", ny, steps).astype(jnp.float32)
        q_cols = w_query.shape[1]
        w_head, moments = fetch(
            w_query, 0, whole_tiles(q_cols * 8 // 16), partial_moments, steps[0]
        )
        others, moments = lax.optimization_barrier(
            (exchange([partial_moments] * nx, "gx", nx)[1:], moments)
        )
        moments = sum(others, moments)
        row_mean = moments[:, 0] / D
        row_var = moments[:, 1] / D - row_mean * row_mean
        normed = (
            (as_float - row_mean[:, None])
            * lax.rsqrt(row_var + 1e-06)[:, None]
            * ln_gain.astype(jnp.float32)
        ).astype(jnp.bfloat16)
        kv_cols = w_keyval.shape[1] // ny
        projected = project(normed, w_head, w_query, w_keyval, kv_cols, "gy", "gx", nx)
        cut = whole_tiles(w_out.shape[1] * 7 // 10)
        parts = exchange(projected, "gx", nx)[1:]
        w_right, part = set_aside(w_out, cut, projected[0])
        parts = [parts[m - 1] for m in order_of(nx)]
        parts, part = lax.optimization_barrier((parts, part))
        part = combine([(part, parts)])
        mixed = exchange([rows_of(part, gy ^ m, ny) for m in range(ny)], "gy", ny)
        order = order_of(ny)
        arrived = lax.optimization_barrier([mixed[m] for m in order])
        mixed = mixed[:1] + [arrived[order.index(m)] for m in range(1, ny)]
        queries = jnp.concatenate(
            [x[:, :q_cols].reshape(seqs, -1, head_dim) for x in mixed], axis=1
        )
        keyval = in_order([x[:, q_cols:][None] for x in mixed], "gy")
        keyval = keyval.transpose(1, 0, 2).reshape(seqs, -1)
        attended = attend_local(
            queries, keyval[:, :head_dim], keyval[:, head_dim:], k_cache, v_cache, cache_lengths
        )
        heads = attended.shape[1] // ny
        returned = in_order(
            exchange(
                [attended[:, m * heads : (m + 1) * heads].reshape(seqs, -1) for m in range(ny)],
                "gy",
                ny,
            ),
            "gy",
        )
        w_left, own = fetch(w_out, 0, cut, returned)
        others = exchange([returned] * nx, "gx", nx)
        order = order_of(nx)
        arrived, own = lax.optimization_barrier(([others[m] for m in order], own))
        arrived = dict(zip(order, arrived))
        everyone = in_order([own] + [arrived[m] for m in range(1, nx)], "gx")
        left = exchange(multiply_held(everyone, w_left, "gy", ny), "gy", ny)
        right = multiply_held(everyone, w_right, "gy", ny)
        right, left[1] = lax.optimization_barrier((right, left[1]))
        right = exchange(right, "gy", ny)
        return combine([(parts[0], parts[1:]) for parts in (left, right)])

    return shards


def solution(mesh):
    placed = (
        P(("groups", "gy"), "gx"),
        P("gx"),
        P("gx", "gy"),
        P("gx", None),
        P("gy", "gx"),
        P(("groups", "gx", "gy"), None, None),
        P(("groups", "gx", "gy"), None, None),
        P(("groups", "gx", "gy")),
    )
    return jax.shard_map(
        make(mesh.shape["gx"], mesh.shape["gy"]),
        mesh=mesh,
        in_specs=placed,
        out_specs=P(("groups", "gy"), "gx"),
        check_vma=False,
    )
```
